1024 devices in a mesh: row: 32 (over z_lo, y), col: 32 (over z_hi, x, core).
Axes of the slice: x: 4, y: 4, z: 32 (z_hi: 4, z_lo: 8; z = z_hi * 8 + z_lo), core: 2. Of those that a mesh axis runs over, the one named last changes fastest.
Arguments:
- features: bfloat16 [131072, 256], P(('col', 'row')), may hold values from -6 to 6
- tile_values: bfloat16 [32, 32, 24, 128, 128], P('row', 'col'), may hold values from 0.0049743652 to 0.099609375
- tile_rows: int32 [32, 32, 24], P('row', 'col'), may hold values from 0 to 31
- tile_cols: int32 [32, 32, 24], P('row', 'col'), may hold values from 0 to 31
- tile_count: int32 [32, 32], P('row', 'col'), may hold values from 6 to 24, as said below
- weight: bfloat16 [256, 256], replicated, may hold values from -0.375 to 0.375
- out_grad: bfloat16 [131072, 256], P(('row', 'col')), may hold values from -6 to 6
Outputs:
- layer_out: bfloat16 [131072, 256], P(('row', 'col'))
- grad_x: bfloat16 [131072, 256], P(('col', 'row'))
The draws below stay inside these ranges and needn't reach their ends.
Inputs may be any that keep to these rules, and one draw needn't show every extreme that they name: `tile_count`: live tile slots of a block; some block has all 24 slots live.
All inputs are finite; a program needn't handle non-finite values.
Results may differ from the reference program's by a relative error of at most 0.03.
Values may be sent and summed in bfloat16 or wider, within the bound.
A program may use at most 32 MiB of HBM per device.

```python
import math
import jax
import jax.numpy as jnp
from jax import lax

F = 256
TILE = 128
CT = 32
NZ = 24
N_OUT = 131072
N_IN = 131072
N_ROW = 32
N_COL = 32


def draw_tile_count(key, part):
    key = jax.random.fold_in(key, 11)
    first_key, second_key = jax.random.split(key)
    level = jax.random.randint(first_key, (N_ROW, N_COL), 0, 17)
    lowest = NZ // 4
    counts = lowest + (NZ - lowest) * level * level // 256
    chosen = jax.random.randint(second_key, (), 0, N_ROW * N_COL)
    flat_counts = jnp.where(jnp.arange(N_ROW * N_COL) == chosen, NZ, counts.reshape(-1))
    return flat_counts.reshape(N_ROW, N_COL).astype(jnp.int32)


def place_ends(entries, own_key, smallest, largest):
    longest = entries.shape.index(max(entries.shape))
    spots = []
    for shift in (0, 1):
        where = [jax.random.randint(jax.random.fold_in(own_key, axis), (), 0, length) for axis, length in enumerate(entries.shape)]
        where[longest] = (where[longest] + shift) % entries.shape[longest]
        spots.append(tuple(where))
    return entries.at[spots[0]].set(smallest).at[spots[1]].set(largest)


def levels(own_key, dims, pieces, smallest, top_value):
    factor_of, own = 1.0, jax.random.fold_in(own_key, 6)
    for dim, parts in pieces:
        heights = jnp.exp(jax.random.uniform(jax.random.fold_in(own, dim), (parts,), jnp.float32, smallest / len(pieces), top_value / len(pieces)))
        factor_of = factor_of * jnp.repeat(heights, dims[dim] // parts).reshape([-1 if axis == dim else 1 for axis in range(len(dims))])
    return factor_of


def scatter_about(own_key, shape, spread, limit, shards=(), kind=jnp.bfloat16):
    result = jax.random.normal(own_key, shape, jnp.float32) * spread
    if len(shards) > 0:
        result = levels(own_key, shape, shards, -0.22, 0.18) * result
    return jnp.clip(result, min=-limit, max=limit).astype(kind)


def setup_inputs(seed: int = 0) -> dict:
    seeds = jax.random.split(jax.random.key(seed), 8)
    features = scatter_about(seeds[0], (N_IN, F), 1.0, 6.0, ((0, 1024),))
    tile_values = jnp.clip(jnp.exp(math.log(0.099609375) - 2.9969585 * jax.random.uniform(seeds[1], (N_ROW, N_COL, NZ, TILE, TILE), jnp.float32) ** levels(seeds[1], (N_ROW, N_COL, NZ, TILE, TILE), ((0, 32), (1, 32)), -0.2, 0.2)), 0.0049743652, 0.099609375).astype(jnp.bfloat16)
    tile_rows = place_ends(jax.random.randint(seeds[2], (N_ROW, N_COL, NZ), 0, CT), jax.random.fold_in(seeds[2], 1), 0, CT - 1).astype(jnp.int32)
    tile_cols = place_ends(jax.random.randint(seeds[3], (N_ROW, N_COL, NZ), 0, CT), jax.random.fold_in(seeds[3], 1), 0, CT - 1).astype(jnp.int32)
    tile_count = draw_tile_count(jax.random.fold_in(seeds[7], 71), 0)
    weight = scatter_about(seeds[5], (F, F), F ** -0.5, 0.375)
    out_grad = scatter_about(seeds[6], (N_OUT, F), 1.0, 6.0, ((0, 1024),))
    return {"features": features, "tile_values": tile_values, "tile_rows": tile_rows, "tile_cols": tile_cols, "tile_count": tile_count, "weight": weight, "out_grad": out_grad}


def activate(value):
    inner = 0.7978845608 * (value + 0.044715 * value * value * value)
    return 0.5 * value * (1.0 + jnp.tanh(inner))

def masked_tiles(tile_values, tile_count, i, j):
    live_mask = jnp.arange(NZ) < tile_count[i, j]
    values = tile_values[i, j].astype(jnp.float32)
    return jnp.where(live_mask[:, None, None], values, jnp.float32(0.0))

def rounded_block(products, indices):
    block = jnp.zeros((CT, TILE, F), jnp.float32).at[indices].add(products)
    block = lax.optimization_barrier(block.astype(jnp.bfloat16))
    return block.astype(jnp.float32)

def reference(features, tile_values, tile_rows, tile_cols, tile_count, weight, out_grad):
    block_len = CT * TILE
    source_blocks = features.reshape(N_COL, CT, TILE, F)

    def row_block(i):

        def step(total, j):
            values = masked_tiles(tile_values, tile_count, i, j)
            sources = source_blocks[j][tile_cols[i, j]].astype(jnp.float32)
            products = jnp.einsum('kab,kbf->kaf', values, sources)
            return (total + rounded_block(products, tile_rows[i, j]), None)
        total, unused = lax.scan(step, jnp.zeros((CT, TILE, F), jnp.float32), jnp.arange(N_COL))
        return total
    aggregated = lax.map(row_block, jnp.arange(N_ROW)).reshape(N_ROW * block_len, F).astype(jnp.bfloat16)
    preact = jnp.dot(aggregated, weight, preferred_element_type=jnp.float32)
    activated, pullback = jax.vjp(activate, preact)
    layer_out = activated.astype(jnp.bfloat16)
    pre_grad = pullback(out_grad.astype(preact.dtype))[0].astype(jnp.bfloat16)
    projected = jnp.dot(pre_grad, weight.T, preferred_element_type=jnp.float32).astype(jnp.bfloat16)
    grad_blocks = projected.reshape(N_ROW, CT, TILE, F)

    def col_block(j):

        def step(total, i):
            values = masked_tiles(tile_values, tile_count, i, j)
            grads = grad_blocks[i][tile_rows[i, j]].astype(jnp.float32)
            products = jnp.einsum('kab,kaf->kbf', values, grads)
            return (total + rounded_block(products, tile_cols[i, j]), None)
        total, unused = lax.scan(step, jnp.zeros((CT, TILE, F), jnp.float32), jnp.arange(N_ROW))
        return total
    grad_x = lax.map(col_block, jnp.arange(N_COL)).reshape(N_COL * block_len, F).astype(jnp.bfloat16)
    return (layer_out, grad_x)
```

```python
import functools

import jax
import jax.numpy as jnp
from jax import lax
from jax.experimental import pallas as pl
from jax.experimental.pallas import tpu as pltpu
from jax.sharding import PartitionSpec as P

MESH = pl.DeviceIdType.MESH
F32 = jnp.float32
BF16 = jnp.bfloat16
NY, NX, NH, NP = 4, 4, 4, 8


def div(a, b):
    return lax.div(a, jnp.int32(b))


def rem(a, b):
    return lax.rem(a, jnp.int32(b))


class Spot:
    def __init__(self):
        self.row, self.col = lax.axis_index("row"), lax.axis_index("col")
        z = div(self.row, NY)
        odd = rem(z, 2)
        self.p = (1 - odd) * div(z, 2) + odd * div(15 - z, 2)
        self.y = rem(self.row, NY)
        self.h = div(self.col, NX * 2)
        self.x = rem(div(self.col, 2), NX)
        self.core = rem(self.col, 2)

    def row_of(self, dp, dy):
        p = rem(self.p + (dp + NP), NP)
        high = div(p, 4)
        z = (1 - high) * (2 * p) + high * (15 - 2 * p)
        return z * NY + rem(self.y + (dy + NY), NY)

    def row_device(self, dp, dy):
        return (self.row_of(dp, dy), self.col)

    def h_of(self, dh):
        return rem(self.h + (dh + NH), NH)

    def x_of(self, dx):
        return rem(self.x + (dx + NX), NX)

    def col_device(self, dh, dx, dcore):
        core = self.core if dcore == 0 else 1 - self.core
        return (self.row, (self.h_of(dh) * NX + self.x_of(dx)) * 2 + core)

    def row_neighbours(self):
        return [self.row_device(*d) for d in ((1, 0), (-1, 0), (0, 1), (0, -1))]

    def col_neighbours(self):
        steps = ((1, 0, 0), (-1, 0, 0), (0, 1, 0), (0, -1, 0), (0, 0, 1))
        return [self.col_device(*d) for d in steps]


def greet(neighbours):
    barrier = pltpu.get_barrier_semaphore()
    for device in neighbours:
        pl.semaphore_signal(barrier, inc=1, device_id=device, device_id_type=MESH)
    pl.semaphore_wait(barrier, len(neighbours))


class Wire:
    def __init__(self, send, recv):
        self.send, self.recv, self.started = send, recv, []

    def go(self, src, dst, device):
        n = len(self.started)
        copy = pltpu.make_async_remote_copy(
            src_ref=src,
            dst_ref=dst,
            send_sem=self.send.at[n],
            recv_sem=self.recv.at[n],
            device_id=device,
            device_id_type=MESH,
        )
        copy.start()
        self.started.append(copy)
        return copy

    def drain(self):
        for copy in self.started:
            copy.wait_send()


def halves(rows):
    return pl.ds(0, rows // 2), pl.ds(rows // 2, rows // 2)


GATHER_ROW_COPIES = 8 + 8 * 4


def gather_row(wire, at, own, block):
    top, low = halves(own.shape[0])
    right, left = at.row_device(1, 0), at.row_device(-1, 0)
    up, down = at.row_device(0, 1), at.row_device(0, -1)

    def spread(dp, src):
        place = block.at[at.row_of(dp, 0)]
        return dp, wire.go(src, place, up), wire.go(src, place, down)

    def pass_on(item):
        dp, from_below, from_above = item
        from_below.wait_recv()
        part = block.at[at.row_of(dp, -1), top]
        a = wire.go(part, part, up)
        from_above.wait_recv()
        part = block.at[at.row_of(dp, 1), low]
        return a, wire.go(part, part, down)

    mine = at.row_of(0, 0)
    fwd = wire.go(own, block.at[mine], right)
    bwd = wire.go(own, block.at[mine], left)
    spreading = [spread(0, own)]
    block[mine] = own[...]
    ends = []
    for s in (1, 2, 3):
        now = []
        fwd.wait_recv()
        t = at.row_of(-s, 0)
        part = block.at[t] if s < 3 else block.at[t, top]
        fwd = wire.go(part, part, right)
        now.append(spread(-s, block.at[t]))
        bwd.wait_recv()
        t = at.row_of(s, 0)
        part = block.at[t] if s < 3 else block.at[t, low]
        bwd = wire.go(part, part, left)
        now.append(spread(s, block.at[t]))
        ends += [pass_on(item) for item in spreading]
        spreading = now
    fwd.wait_recv()
    bwd.wait_recv()
    now = [spread(4, block.at[at.row_of(4, 0)])]
    ends += [pass_on(item) for item in spreading + now]
    for a, b in ends:
        a.wait_recv()
        b.wait_recv()


class Ring4:
    def __init__(self, wire, part, up, down, first_in, held, second_in):
        self.wire, self.part, self.up, self.down = wire, part, up, down
        self.first_in, self.held, self.second_in = first_in, held, second_in
        self.one, self.two = {}, {}
        self.top, self.low = halves(held.shape[2])

    def first(self, i):
        far = self.part(i, 2)
        self.one[i] = (
            self.wire.go(far.at[self.top], self.first_in.at[i, 0], self.up),
            self.wire.go(far.at[self.low], self.first_in.at[i, 1], self.down),
        )

    def second(self, i):
        top, low = self.top, self.low
        near = self.part(i, 1)
        self.held[i, 0, low] = near[low]
        self.one[i][0].wait_recv()
        self.held[i, 0, top] = add(near[top], self.first_in[i, 0])
        a = self.wire.go(self.held.at[i, 0], self.second_in.at[i, 0], self.up)
        near = self.part(i, -1)
        self.held[i, 1, top] = near[top]
        self.one[i][1].wait_recv()
        self.held[i, 1, low] = add(near[low], self.first_in[i, 1])
        self.two[i] = (a, self.wire.go(self.held.at[i, 1], self.second_in.at[i, 1], self.down))

    def third(self, i):
        for copy in self.two[i]:
            copy.wait_recv()
        return add3(self.part(i, 0)[...], self.second_in[i, 0], self.second_in[i, 1])


def add(a, b):
    return (a.astype(F32) + b.astype(F32)).astype(BF16)


def add3(a, b, c):
    return a.astype(F32) + b.astype(F32) + c.astype(F32)


SUM_ROW_COPIES = 8 * 4 + 8


def sum_row(wire, at, partial, out, first_in, held, second_in, half_in, half_out, full_in, full_out):
    order = (4, 3, -3, 2, -2, 1, -1, 0)
    rows = out.shape[0]
    mid = rows // 2
    right, left = at.row_device(1, 0), at.row_device(-1, 0)
    ring = Ring4(
        wire,
        lambda i, dy: partial.at[at.row_of(order[i], dy)],
        at.row_device(0, 1),
        at.row_device(0, -1),
        first_in,
        held,
        second_in,
    )
    last = {}

    def along_z(i, value):
        dp = order[i]
        if dp == 4:
            half_out[...] = value.astype(BF16)
            last[1] = wire.go(half_out.at[pl.ds(0, mid)], half_in.at[0], right)
            last[-1] = wire.go(half_out.at[pl.ds(mid, mid)], half_in.at[1], left)
        elif dp == 0:
            last[1].wait_recv()
            last[-1].wait_recv()
            out[...] = add3(value, full_in[2, 0], full_in[2, 1]).astype(BF16)
        else:
            way, step = (1, 0) if dp > 0 else (-1, 1)
            s = 3 - abs(dp)
            last[way].wait_recv()
            if s == 0:
                lo, hi = (0, mid) if way > 0 else (mid, rows)
                keep = (mid, rows) if way > 0 else (0, mid)
                full_out[s, step, lo:hi] = (value[lo:hi] + half_in[step].astype(F32)).astype(BF16)
                full_out[s, step, keep[0] : keep[1]] = value[keep[0] : keep[1]].astype(BF16)
            else:
                full_out[s, step] = (value + full_in[s - 1, step].astype(F32)).astype(BF16)
            last[way] = wire.go(full_out.at[s, step], full_in.at[s, step], right if way > 0 else left)

    ring.first(0)
    for t in range(len(order) + 1):
        if t + 1 < len(order):
            ring.first(t + 1)
        if t < len(order):
            ring.second(t)
        if t >= 1:
            along_z(t - 1, ring.third(t - 1))


def sum_row_scratch(rows, width):
    return [
        pltpu.VMEM((8, 2, rows // 2, width), BF16),
        pltpu.VMEM((8, 2, rows, width), BF16),
        pltpu.VMEM((8, 2, rows, width), BF16),
        pltpu.VMEM((2, rows // 2, width), BF16),
        pltpu.VMEM((rows, width), BF16),
        pltpu.VMEM((3, 2, rows, width), BF16),
        pltpu.VMEM((3, 2, rows, width), BF16),
    ]


SUM_COL_COPIES = 4 + 4 * 4 + 4


def sum_col(wire, at, partial, pair_in, paired, first_in, held, second_in, half_in, half_out, full_in, full_out):
    order = (2, 1, -1, 0)
    rows = partial.shape[3]
    mid = rows // 2
    right, left = at.col_device(1, 0, 0), at.col_device(-1, 0, 0)
    other = at.col_device(0, 0, 1)
    arriving = [
        wire.go(partial.at[at.h_of(dh), :, 1 - at.core], pair_in.at[i], other)
        for i, dh in enumerate(order)
    ]
    ring = Ring4(
        wire,
        lambda i, dx: paired.at[i, at.x_of(dx)],
        at.col_device(0, 1, 0),
        at.col_device(0, -1, 0),
        first_in,
        held,
        second_in,
    )

    def pair(i):
        arriving[i].wait_recv()
        paired[i] = add(partial[at.h_of(order[i]), :, at.core], pair_in[i])

    pair(0)
    ring.first(0)
    total, last = None, {}
    for t in range(5):
        if t + 1 < 4:
            pair(t + 1)
            ring.first(t + 1)
        if t < 4:
            ring.second(t)
        if t == 0:
            continue
        value = ring.third(t - 1)
        if t == 1:
            half_out[...] = value.astype(BF16)
            last[1] = wire.go(half_out.at[pl.ds(0, mid)], half_in.at[0], right)
            last[-1] = wire.go(half_out.at[pl.ds(mid, mid)], half_in.at[1], left)
        elif t < 4:
            full_out[t - 2] = value
        else:
            total = value
    last[1].wait_recv()
    full_in_f = wire_full(wire, full_out, half_in, full_in, 0, 0, mid, rows, right)
    last[-1].wait_recv()
    full_in_b = wire_full(wire, full_out, half_in, full_in, 1, mid, mid, rows, left)
    full_in_f.wait_recv()
    full_in_b.wait_recv()
    return add3(total, full_in[0], full_in[1])


def wire_full(wire, full_out, half_in, full_in, step, start, mid, rows, device):
    lo, keep = (slice(0, mid), slice(mid, rows)) if step == 0 else (slice(mid, rows), slice(0, mid))
    sent = full_in.at[2 + step]
    full_in[2 + step, lo] = (full_out[step, lo] + half_in[step].astype(F32)).astype(BF16)
    full_in[2 + step, keep] = full_out[step, keep].astype(BF16)
    return wire.go(sent, full_in.at[step], device)


def sum_col_scratch(rows, width):
    return [
        pltpu.VMEM((4, 4, rows, width), BF16),
        pltpu.VMEM((4, 4, rows, width), BF16),
        pltpu.VMEM((4, 2, rows // 2, width), BF16),
        pltpu.VMEM((4, 2, rows, width), BF16),
        pltpu.VMEM((4, 2, rows, width), BF16),
        pltpu.VMEM((2, rows // 2, width), BF16),
        pltpu.VMEM((rows, width), BF16),
        pltpu.VMEM((4, rows, width), BF16),
        pltpu.VMEM((2, rows, width), F32),
    ]


GATHER_COL_COPIES = 4 + 2 + 3 * 4 + 2 * 2 + 2 + 4


def gather_col(wire, at, own, block):
    rows = own.shape[0]
    top, low = halves(rows)
    right, left = at.col_device(1, 0, 0), at.col_device(-1, 0, 0)
    up, down = at.col_device(0, 1, 0), at.col_device(0, -1, 0)
    other = at.col_device(0, 0, 1)

    def place(dh, dx, part=None):
        ref = block.at[at.h_of(dh), at.x_of(dx), at.core]
        return ref if part is None else ref.at[part]

    block[at.h, at.x, at.core] = own[...]
    fwd_top = wire.go(own.at[top], place(0, 0, top), right)
    bwd_low = wire.go(own.at[low], place(0, 0, low), left)
    fwd_low = wire.go(own.at[low], place(0, 0, low), right)
    bwd_top = wire.go(own.at[top], place(0, 0, top), left)

    def spread(dh, src, part=None):
        return wire.go(src, place(dh, 0, part), up), wire.go(src, place(dh, 0, part), down)

    def pass_on(dh, item):
        item[0].wait_recv()
        part = place(dh, -1, top)
        a = wire.go(part, part, up)
        item[1].wait_recv()
        part = place(dh, 1, low)
        return a, wire.go(part, part, down)

    def across(dh, copies):
        for copy in copies:
            copy.wait_recv()
        part = block.at[at.h_of(dh), :, at.core]
        return wire.go(part, part, other)

    here = spread(0, own)
    here = pass_on(0, here)
    fwd_top.wait_recv()
    far_top = wire.go(place(-1, 0, top), place(-1, 0, top), right)
    bwd_low.wait_recv()
    far_low = wire.go(place(1, 0, low), place(1, 0, low), left)
    across_copies = [across(0, here)]
    fwd_low.wait_recv()
    behind = spread(-1, place(-1, 0))
    bwd_top.wait_recv()
    ahead = spread(1, place(1, 0))
    behind = pass_on(-1, behind)
    ahead = pass_on(1, ahead)
    across_copies.append(across(-1, behind))
    across_copies.append(across(1, ahead))
    far_top.wait_recv()
    tops = spread(2, place(2, 0, top), top)
    far_low.wait_recv()
    lows = spread(2, place(2, 0, low), low)
    tops[0].wait_recv()
    part = place(2, -1, top)
    a = wire.go(part, part, up)
    lows[1].wait_recv()
    part = place(2, 1, low)
    b = wire.go(part, part, down)
    across_copies.append(across(2, (tops[1], lows[0], a, b)))
    for copy in across_copies:
        copy.wait_recv()


def k_gather_row(own, block, send, recv):
    at = Spot()
    greet(at.row_neighbours())
    wire = Wire(send, recv)
    gather_row(wire, at, own, block)
    wire.drain()


def k_sum_row(partial, out, *scratch):
    *buffers, send, recv = scratch
    at = Spot()
    greet(at.row_neighbours())
    wire = Wire(send, recv)
    sum_row(wire, at, partial, out, *buffers)
    wire.drain()


def dense(aggregated, weight, out_grad, layer_out):
    v = jnp.dot(aggregated, weight[...], preferred_element_type=F32)
    c, d = 0.7978845608, 0.044715
    th = jnp.tanh(c * (v + d * v * v * v))
    layer_out[...] = (0.5 * v * (1.0 + th)).astype(BF16)
    slope = 0.5 * (1.0 + th) + 0.5 * v * (1.0 - th * th) * (c * (1.0 + (3.0 * d) * v * v))
    pre_grad = (out_grad[...].astype(F32) * slope).astype(BF16)
    return lax.dot_general(
        pre_grad, weight[...], (((1,), (1,)), ((), ())), preferred_element_type=F32
    ).astype(BF16)


def k_middle(partial, weight, out_grad, layer_out, block, projected, *scratch):
    *buffers, send, recv = scratch
    at = Spot()
    greet(at.col_neighbours())
    wire = Wire(send, recv)
    aggregated = sum_col(wire, at, partial, *buffers).astype(BF16)
    projected[...] = dense(aggregated, weight, out_grad, layer_out)
    gather_col(wire, at, projected, block)
    wire.drain()


VMEM_SPEC = pl.BlockSpec(memory_space=pltpu.VMEM)
LIMIT = 48 * 1024 * 1024


def remote(collective_id):
    return pltpu.CompilerParams(
        collective_id=collective_id, has_side_effects=True, vmem_limit_bytes=LIMIT
    )


def sems(n):
    return [pltpu.SemaphoreType.DMA((n,)), pltpu.SemaphoreType.DMA((n,))]


def call_gather_row(own):
    rows, width = own.shape
    return pl.pallas_call(
        k_gather_row,
        out_shape=jax.ShapeDtypeStruct((NP * NY, rows, width), BF16),
        in_specs=[VMEM_SPEC],
        out_specs=VMEM_SPEC,
        scratch_shapes=sems(GATHER_ROW_COPIES),
        compiler_params=remote(0),
        name="gather_row",
    )(own)


def call_sum_row(partial):
    _, rows, width = partial.shape
    return pl.pallas_call(
        k_sum_row,
        out_shape=jax.ShapeDtypeStruct((rows, width), BF16),
        in_specs=[VMEM_SPEC],
        out_specs=VMEM_SPEC,
        scratch_shapes=sum_row_scratch(rows, width) + sems(SUM_ROW_COPIES),
        compiler_params=remote(1),
        name="sum_row",
    )(partial)


def call_middle(partial, weight, out_grad):
    _, rows, width = partial.shape
    layer_out, block = pl.pallas_call(
        k_middle,
        out_shape=(
            jax.ShapeDtypeStruct((rows, width), BF16),
            jax.ShapeDtypeStruct((NH, NX, 2, rows, width), BF16),
        ),
        in_specs=[VMEM_SPEC] * 3,
        out_specs=(VMEM_SPEC, VMEM_SPEC),
        scratch_shapes=[pltpu.VMEM((rows, width), BF16)]
        + sum_col_scratch(rows, width)
        + sems(SUM_COL_COPIES + GATHER_COL_COPIES),
        compiler_params=remote(2),
        name="middle",
    )(partial.reshape(NH, NX, 2, rows, width), weight, out_grad)
    return layer_out, block.reshape(NH * NX * 2, rows, width)


def k_tiles(contract, to, source_at, count, tiles, source, out, total):
    total[...] = jnp.zeros_like(total)

    def slot(k, carry):
        product = lax.dot_general(
            tiles[k],
            source[source_at[k]],
            (((contract,), (0,)), ((), ())),
            preferred_element_type=F32,
        )
        total[to[k]] += product
        return carry

    lax.fori_loop(0, count[0], slot, 0)
    out[...] = total[...].astype(BF16)


def call_tiles(contract, to, source_at, count, tiles, source):
    smem = pl.BlockSpec(memory_space=pltpu.SMEM)
    return pl.pallas_call(
        functools.partial(k_tiles, contract),
        out_shape=jax.ShapeDtypeStruct(source.shape, BF16),
        in_specs=[smem] * 3 + [VMEM_SPEC] * 2,
        out_specs=VMEM_SPEC,
        scratch_shapes=[pltpu.VMEM(source.shape, F32)],
        compiler_params=pltpu.CompilerParams(vmem_limit_bytes=LIMIT),
        name="tiles" + str(contract),
    )(to, source_at, count, tiles, source)


def per_device(features, tile_values, tile_rows, tile_cols, tile_count, weight, out_grad):
    tiles = tile_values[0, 0]
    row_index, col_index, count = tile_rows[0, 0], tile_cols[0, 0], tile_count[0]
    source = call_gather_row(features)
    partial = call_tiles(1, row_index, col_index, count, tiles, source)
    layer_out, grads = call_middle(partial, weight, out_grad)
    back = call_tiles(0, col_index, row_index, count, tiles, grads)
    return layer_out, call_sum_row(back)


def solution(mesh):
    in_specs = (
        P(("col", "row"), None),
        P("row", "col", None, None, None),
        P("row", "col", None),
        P("row", "col", None),
        P("row", "col"),
        P(),
        P(("row", "col"), None),
    )
    out_specs = (P(("row", "col"), None), P(("col", "row"), None))
    return jax.shard_map(
        per_device, mesh=mesh, in_specs=in_specs, out_specs=out_specs, check_vma=False
    )
```

```python
import jax
import jax.numpy as jnp
from jax import lax
from jax.experimental import pallas as pl
from jax.experimental.pallas import tpu as pltpu
from jax.sharding import PartitionSpec as P

MESH = pl.DeviceIdType.MESH
F32 = jnp.float32
BF16 = jnp.bfloat16
NY, NX, NH, NP = 4, 4, 4, 8
ROWS = NP * NY
COLS = NH * NX * 2


def div(a, b):
    return lax.div(a, jnp.int32(b))


def rem(a, b):
    return lax.rem(a, jnp.int32(b))


class Spot:
    def __init__(self):
        self.row, self.col = lax.axis_index("row"), lax.axis_index("col")
        z = div(self.row, NY)
        odd = rem(z, 2)
        self.p = (1 - odd) * div(z, 2) + odd * div(15 - z, 2)
        self.y = rem(self.row, NY)
        self.h = div(self.col, NX * 2)
        self.x = rem(div(self.col, 2), NX)
        self.core = rem(self.col, 2)

    def row_of(self, dp, dy):
        p = rem(self.p + (dp + NP), NP)
        high = div(p, 4)
        z = (1 - high) * (2 * p) + high * (15 - 2 * p)
        return z * NY + rem(self.y + (dy + NY), NY)

    def row_device(self, dp, dy):
        return (self.row_of(dp, dy), self.col)

    def h_of(self, dh):
        return rem(self.h + (dh + NH), NH)

    def x_of(self, dx):
        return rem(self.x + (dx + NX), NX)

    def col_device(self, dh, dx, dcore):
        core = self.core if dcore == 0 else 1 - self.core
        return (self.row, (self.h_of(dh) * NX + self.x_of(dx)) * 2 + core)

    def slot(self, dh, dx, dcore=0):
        core = self.core if dcore == 0 else 1 - self.core
        return core * (NH * NX) + self.h_of(dh) * NX + self.x_of(dx)

    def row_neighbours(self):
        return [self.row_device(*d) for d in ((1, 0), (-1, 0), (0, 1), (0, -1), (0, 2))]

    def col_neighbours(self):
        steps = ((1, 0, 0), (-1, 0, 0), (0, 1, 0), (0, -1, 0), (0, 2, 0), (0, 0, 1))
        return [self.col_device(*d) for d in steps]


def greet(neighbours):
    barrier = pltpu.get_barrier_semaphore()
    for device in neighbours:
        pl.semaphore_signal(barrier, inc=1, device_id=device, device_id_type=MESH)
    pl.semaphore_wait(barrier, len(neighbours))


class Wire:
    def __init__(self, send, recv):
        self.send, self.recv, self.started = send, recv, []

    def go(self, src, dst, device):
        n = len(self.started)
        copy = pltpu.make_async_remote_copy(
            src_ref=src,
            dst_ref=dst,
            send_sem=self.send.at[n],
            recv_sem=self.recv.at[n],
            device_id=device,
            device_id_type=MESH,
        )
        copy.start()
        self.started.append(copy)
        return copy

    def drain(self):
        for copy in self.started:
            copy.wait_send()


def halves(rows):
    return pl.ds(0, rows // 2), pl.ds(rows // 2, rows // 2)


GATHER_ROW_COPIES = 14 + 5 * 6 + 3 * 6


def gather_row(wire, at, own, block):
    part = halves(own.shape[0])
    along = (at.row_device(1, 0), at.row_device(-1, 0))
    up, down, far = at.row_device(0, 1), at.row_device(0, -1), at.row_device(0, 2)

    def place(dp, dy, half):
        return block.at[at.row_of(dp, dy), part[half]]

    ends = []

    def spread(dp, half, src, direct):
        dst = place(dp, 0, half)
        a, b = wire.go(src, dst, up), wire.go(src, dst, down)
        if direct:
            ends.extend((a, b, wire.go(src, dst, far)))
            return None
        return dp, half, a, b

    def pass_on(item):
        dp, half, a, b = item
        if half == 0:
            a.wait_recv()
            ref = place(dp, -1, 0)
            ends.extend((b, wire.go(ref, ref, up)))
        else:
            b.wait_recv()
            ref = place(dp, 1, 1)
            ends.extend((a, wire.go(ref, ref, down)))

    moving = {}
    for half in (0, 1):
        for way in (0, 1):
            now = half if way == 0 else 1 - half
            moving[way, now] = wire.go(own.at[part[now]], place(0, 0, now), along[way])
    spreading = [spread(0, half, own.at[part[half]], False) for half in (0, 1)]
    block[at.row_of(0, 0)] = own[...]
    for s in (1, 2, 3, 4):
        now = []
        for half in (0, 1):
            for way in (0, 1):
                part_now = half if way == 0 else 1 - half
                copy = moving.pop((way, part_now), None)
                if copy is None:
                    continue
                copy.wait_recv()
                dp = -s if way == 0 else s
                ref = place(dp, 0, part_now)
                if s < 3 or (s == 3 and part_now == way):
                    moving[way, part_now] = wire.go(ref, ref, along[way])
                now.append(spread(dp, part_now, ref, s >= 3))
        for item in spreading:
            if item is not None:
                pass_on(item)
        spreading = now
    for copy in ends:
        copy.wait_recv()


def add(a, b):
    return (a.astype(F32) + b.astype(F32)).astype(BF16)


SUM_ROW_COPIES = 3 * 3 + 5 * 6 + 14
DIRECT = 3


def sum_row(wire, at, block_of, out, mine, direct_in, first_in, held, second_in, total, z_in, z_out):
    order = (4, 3, -3, 2, -2, 1, -1, 0)
    rows = out.shape[0]
    cut = (slice(0, rows // 2), slice(rows // 2, rows))
    part = halves(rows)
    along = (at.row_device(1, 0), at.row_device(-1, 0))
    up, down, far = at.row_device(0, 1), at.row_device(0, -1), at.row_device(0, 2)
    flight = {}

    def first(i):
        for dy in (2, 1, -1):
            mine[i, dy % NY] = block_of(at.row_of(order[i], dy)).astype(BF16)
        if i < DIRECT:
            flight[i] = (
                wire.go(mine.at[i, 2], direct_in.at[i, 2], far),
                wire.go(mine.at[i, 1], direct_in.at[i, 0], up),
                wire.go(mine.at[i, 3], direct_in.at[i, 1], down),
            )
            return
        k = i - DIRECT
        flight[i] = [
            wire.go(mine.at[i, 2, part[0]], first_in.at[k, 0], up),
            wire.go(mine.at[i, 2, part[1]], first_in.at[k, 1], down),
            wire.go(mine.at[i, 1, part[1]], second_in.at[k, 0, part[1]], up),
            wire.go(mine.at[i, 3, part[0]], second_in.at[k, 1, part[0]], down),
        ]

    def second(i):
        k = i - DIRECT
        flight[i][0].wait_recv()
        held[k, 0] = add(mine[i, 1, cut[0]], first_in[k, 0])
        flight[i].append(wire.go(held.at[k, 0], second_in.at[k, 0, part[0]], up))
        flight[i][1].wait_recv()
        held[k, 1] = add(mine[i, 3, cut[1]], first_in[k, 1])
        flight[i].append(wire.go(held.at[k, 1], second_in.at[k, 1, part[1]], down))

    def third(i):
        value = block_of(at.row_of(order[i], 0))
        if i < DIRECT:
            for copy in flight[i]:
                copy.wait_recv()
            for n in range(3):
                value += direct_in[i, n].astype(F32)
        else:
            for copy in flight[i][2:]:
                copy.wait_recv()
            for n in range(2):
                value += second_in[i - DIRECT, n].astype(F32)
        total[i] = value

    moving = {}

    def send(way, half, step):
        moving[way, half] = wire.go(z_out.at[way, half, step], z_in.at[way, half, step], along[way])

    def start(i, way, half, step):
        z_out[way, half, step] = total[i, cut[half]].astype(BF16)
        send(way, half, step)

    def carry(i, way, half, step):
        moving[way, half].wait_recv()
        z_out[way, half, step] = (total[i, cut[half]] + z_in[way, half, step - 1].astype(F32)).astype(BF16)
        send(way, half, step)

    for i in range(4):
        first(i)
    third(0)
    start(0, 0, 0, 0)
    start(0, 1, 1, 0)
    first(4)
    third(1)
    start(1, 0, 1, 1)
    third(2)
    start(2, 1, 0, 1)
    first(5)
    second(3)
    carry(1, 0, 0, 1)
    carry(2, 1, 1, 1)
    first(6)
    second(4)
    first(7)
    third(3)
    third(4)
    for step, i in ((2, 3), (3, 5)):
        for half in (0, 1):
            carry(i, 0, 1 - half, step)
            carry(i + 1, 1, half, step)
        if step == 2:
            for n in (5, 6, 7):
                second(n)
            third(5)
            third(6)
    third(7)
    for half in (0, 1):
        value = total[7, cut[half]]
        for way in (0, 1):
            moving[way, half].wait_recv()
            value += z_in[way, half, 3].astype(F32)
        out[cut[half]] = value.astype(BF16)


def sum_row_scratch(rows, width):
    mid = rows // 2
    return [
        pltpu.VMEM((8, 4, rows, width), BF16),
        pltpu.VMEM((DIRECT, 3, rows, width), BF16),
        pltpu.VMEM((8 - DIRECT, 2, mid, width), BF16),
        pltpu.VMEM((8 - DIRECT, 2, mid, width), BF16),
        pltpu.VMEM((8 - DIRECT, 2, rows, width), BF16),
        pltpu.VMEM((8, rows, width), F32),
        pltpu.VMEM((2, 2, 4, mid, width), BF16),
        pltpu.VMEM((2, 2, 4, mid, width), BF16),
    ]


SUM_COL_COPIES = 4 + 4 * 3 + 6


def sum_col(wire, at, block_of, pair_out, pair_in, paired, x_in, total, z_in, z_out):
    order = (2, 1, -1, 0)
    rows = total.shape[1]
    mid = rows // 2
    cut = (slice(0, mid), slice(mid, rows))
    part = halves(rows)
    along = (at.col_device(1, 0, 0), at.col_device(-1, 0, 0))
    up, down, far = at.col_device(0, 1, 0), at.col_device(0, -1, 0), at.col_device(0, 2, 0)
    other = at.col_device(0, 0, 1)
    crossing, flight = [], []
    for i, dh in enumerate(order):
        for dx in range(NX):
            pair_out[i, dx] = block_of(at.slot(dh, dx, 1)).astype(BF16)
        crossing.append(wire.go(pair_out.at[i], pair_in.at[i], other))
    for i, dh in enumerate(order):
        crossing[i].wait_recv()
        copies = []
        for dx, n, device in ((2, 2, far), (1, 0, up), (3, 1, down)):
            paired[i, dx] = add(block_of(at.slot(dh, dx)), pair_in[i, dx])
            copies.append(wire.go(paired.at[i, dx], x_in.at[i, n], device))
        flight.append(copies)

    def third(i):
        value = block_of(at.slot(order[i], 0)) + pair_in[i, 0].astype(F32)
        for copy in flight[i]:
            copy.wait_recv()
        for n in range(3):
            value += x_in[i, n].astype(F32)
        total[i] = value

    moving = {}

    def send(way, half, step):
        moving[way, half] = wire.go(z_out.at[way, half, step], z_in.at[way, half, step], along[way])

    def start(i, way, half, step):
        z_out[way, half, step] = total[i, cut[half]].astype(BF16)
        send(way, half, step)

    def carry(i, way, half, step):
        moving[way, half].wait_recv()
        z_out[way, half, step] = (total[i, cut[half]] + z_in[way, half, step - 1].astype(F32)).astype(BF16)
        send(way, half, step)

    third(0)
    start(0, 0, 0, 0)
    start(0, 1, 1, 0)
    third(1)
    start(1, 0, 1, 1)
    third(2)
    start(2, 1, 0, 1)
    third(3)
    carry(1, 0, 0, 1)
    carry(2, 1, 1, 1)
    for half in (0, 1):
        value = total[3, cut[half]]
        for way in (0, 1):
            moving[way, half].wait_recv()
            value += z_in[way, half, 1].astype(F32)
        total[3, cut[half]] = value
    return total[3]


def sum_col_scratch(rows, width):
    mid = rows // 2
    return [
        pltpu.VMEM((4, 4, rows, width), BF16),
        pltpu.VMEM((4, 4, rows, width), BF16),
        pltpu.VMEM((4, 4, rows, width), BF16),
        pltpu.VMEM((4, 3, rows, width), BF16),
        pltpu.VMEM((4, rows, width), F32),
        pltpu.VMEM((2, 2, 2, mid, width), BF16),
        pltpu.VMEM((2, 2, 2, mid, width), BF16),
    ]


GATHER_COL_COPIES = 6 + 8 * 3 + 8


def gather_col(wire, at, own, block):
    part = halves(own.shape[0])
    along = (at.col_device(1, 0, 0), at.col_device(-1, 0, 0))
    near = (at.col_device(0, 2, 0), at.col_device(0, 1, 0), at.col_device(0, -1, 0))
    other = at.col_device(0, 0, 1)

    def place(dh, half):
        return block.at[at.slot(dh, 0), part[half]]

    moving = {}
    for way, half in ((0, 0), (1, 1), (0, 1), (1, 0)):
        moving[way, half] = wire.go(own.at[part[half]], place(0, half), along[way])
    block[at.slot(0, 0)] = own[...]

    def spread(dh, half):
        ref = place(dh, half)
        return dh, half, [wire.go(ref, ref, device) for device in near]

    crossed = []

    def across(item):
        dh, half, copies = item
        for copy in copies:
            copy.wait_recv()
        first = at.core * (NH * NX) + at.h_of(dh) * NX
        ref = block.at[pl.ds(first, NX), part[half]]
        crossed.append(wire.go(ref, ref, other))

    def arrive(way, half, dh):
        moving[way, half].wait_recv()
        if abs(dh) == 1 and half == way:
            ref = place(dh, half)
            moving[way, half] = wire.go(ref, ref, along[way])
        return spread(dh, half)

    here = [spread(0, half) for half in (0, 1)]
    for item in here:
        across(item)
    early = [arrive(0, 0, -1), arrive(1, 1, 1)]
    late = [arrive(0, 1, -1), arrive(1, 0, 1)]
    for item in early:
        across(item)
    last = [arrive(0, 0, 2)]
    for item in late:
        across(item)
    last.append(arrive(1, 1, 2))
    for item in last:
        across(item)
    for copy in crossed:
        copy.wait_recv()


def dense(aggregated, weight, out_grad, layer_out):
    v = jnp.dot(aggregated, weight[...], preferred_element_type=F32)
    c, d = 0.7978845608, 0.044715
    th = jnp.tanh(c * (v + d * v * v * v))
    layer_out[...] = (0.5 * v * (1.0 + th)).astype(BF16)
    slope = 0.5 * (1.0 + th) + 0.5 * v * (1.0 - th * th) * (c * (1.0 + (3.0 * d) * v * v))
    pre_grad = (out_grad[...].astype(F32) * slope).astype(BF16)
    return lax.dot_general(
        pre_grad, weight[...], (((1,), (1,)), ((), ())), preferred_element_type=F32
    ).astype(BF16)


def tile_sums(contract, tiles, source, source_at, before, sums):
    slots = tiles.shape[0]
    group = 4

    def some(g, carry):
        for n in range(group):
            k = g * group + n
            product = lax.dot_general(
                tiles[k],
                source[source_at[k]],
                (((contract,), (0,)), ((), ())),
                preferred_element_type=F32,
            )
            sums[k] = product + sums[before[k]]
        return carry

    lax.fori_loop(0, slots // group, some, 0)


def k_plan(rows, cols, count, row_slot, row_before, row_last, col_before, col_last):
    slots = rows.shape[0]

    def clear(t, carry):
        row_last[t] = jnp.int32(slots)
        col_last[t] = jnp.int32(slots)
        return carry

    lax.fori_loop(0, ROWS, clear, 0)

    def slot(k, carry):
        r, c = rows[k], cols[k]
        s = rem(r, 2) * (NH * NX) + div(r, 2)
        row_slot[k] = s
        live = k < count[0]
        old_row, old_col = row_last[s], col_last[c]
        row_before[k], col_before[k] = old_row, old_col
        row_last[s] = jnp.where(live, k, old_row)
        col_last[c] = jnp.where(live, k, old_col)
        return carry

    lax.fori_loop(0, slots, slot, 0)


SMEM_SPEC = pl.BlockSpec(memory_space=pltpu.SMEM)
VMEM_SPEC = pl.BlockSpec(memory_space=pltpu.VMEM)
ANY_SPEC = pl.BlockSpec(memory_space=pl.ANY)
LIMIT = 56 * 1024 * 1024


def plan(rows, cols, count):
    slots = rows.shape[0]
    one = jax.ShapeDtypeStruct((slots,), jnp.int32)
    table = jax.ShapeDtypeStruct((ROWS,), jnp.int32)
    return pl.pallas_call(
        k_plan,
        out_shape=(one, one, table, one, table),
        in_specs=[SMEM_SPEC] * 3,
        out_specs=(SMEM_SPEC,) * 5,
        name="plan",
    )(rows, cols, count)


def k_layer(
    col_at, row_slot, row_before, row_last, col_before, col_last,
    own, tiles_hbm, weight, out_grad, layer_out, grad_x, *scratch
):
    tiles, tile_sem, source, grads, projected, sums, *scratch = scratch
    n_row, n_col = len(sum_row_scratch(32, 128)), len(sum_col_scratch(32, 128))
    row_buffers, col_buffers = scratch[:n_row], scratch[n_row : n_row + n_col]
    send, recv = scratch[n_row + n_col :]
    at = Spot()
    load = pltpu.make_async_copy(tiles_hbm, tiles, tile_sem)
    load.start()
    sums[tiles.shape[0]] = jnp.zeros(sums.shape[1:], F32)
    greet(at.row_neighbours() + at.col_neighbours())
    wire = Wire(send, recv)
    gather_row(wire, at, own, source)
    load.wait()
    tile_sums(1, tiles, source, col_at, row_before, sums)
    aggregated = sum_col(wire, at, lambda slot: sums[row_last[slot]], *col_buffers)
    projected[...] = dense(aggregated.astype(BF16), weight, out_grad, layer_out)
    gather_col(wire, at, projected, grads)
    tile_sums(0, tiles, grads, row_slot, col_before, sums)
    sum_row(wire, at, lambda row: sums[col_last[row]], grad_x, *row_buffers)
    wire.drain()


def layer(tables, own, tiles, weight, out_grad):
    rows, width = own.shape
    slots = tiles.shape[0]
    block = jax.ShapeDtypeStruct((rows, width), BF16)
    copies = GATHER_ROW_COPIES + SUM_COL_COPIES + GATHER_COL_COPIES + SUM_ROW_COPIES
    return pl.pallas_call(
        k_layer,
        out_shape=(block, block),
        in_specs=[SMEM_SPEC] * 6 + [VMEM_SPEC, ANY_SPEC, VMEM_SPEC, VMEM_SPEC],
        out_specs=(VMEM_SPEC, VMEM_SPEC),
        scratch_shapes=[
            pltpu.VMEM(tiles.shape, BF16),
            pltpu.SemaphoreType.DMA,
            pltpu.VMEM((ROWS, rows, width), BF16),
            pltpu.VMEM((COLS, rows, width), BF16),
            pltpu.VMEM((rows, width), BF16),
            pltpu.VMEM((slots + 1, rows, width), F32),
        ]
        + sum_row_scratch(rows, width)
        + sum_col_scratch(rows, width)
        + [pltpu.SemaphoreType.DMA((copies,)), pltpu.SemaphoreType.DMA((copies,))],
        compiler_params=pltpu.CompilerParams(
            collective_id=0, has_side_effects=True, vmem_limit_bytes=LIMIT
        ),
        name="layer",
    )(*tables, own, tiles, weight, out_grad)


def per_device(features, tile_values, tile_rows, tile_cols, tile_count, weight, out_grad):
    rows, cols = tile_rows[0, 0], tile_cols[0, 0]
    tables = plan(rows, cols, tile_count[0])
    return layer((cols,) + tuple(tables), features, tile_values[0, 0], weight, out_grad)


def solution(mesh):
    in_specs = (
        P(("col", "row"), None),
        P("row", "col", None, None, None),
        P("row", "col", None),
        P("row", "col", None),
        P("row", "col"),
        P(),
        P(("row", "col"), None),
    )
    out_specs = (P(("row", "col"), None), P(("col", "row"), None))
    return jax.shard_map(
        per_device, mesh=mesh, in_specs=in_specs, out_specs=out_specs, check_vma=False
    )
```

```python
import jax
import jax.numpy as jnp
from jax import lax
from jax.experimental import pallas as pl
from jax.experimental.pallas import tpu as pltpu
from jax.sharding import PartitionSpec as P

MESH = pl.DeviceIdType.MESH
F32 = jnp.float32
BF16 = jnp.bfloat16
NY, NX, NH, NP = 4, 4, 4, 8
ROWS = NP * NY
COLS = NH * NX * 2


def div(a, b):
    return lax.div(a, jnp.int32(b))


def rem(a, b):
    return lax.rem(a, jnp.int32(b))


class Spot:
    def __init__(self):
        self.row, self.col = lax.axis_index("row"), lax.axis_index("col")
        z = div(self.row, NY)
        odd = rem(z, 2)
        self.p = (1 - odd) * div(z, 2) + odd * div(15 - z, 2)
        self.y = rem(self.row, NY)
        self.h = div(self.col, NX * 2)
        self.x = rem(div(self.col, 2), NX)
        self.core = rem(self.col, 2)

    def row_of(self, dp, dy):
        p = rem(self.p + (dp + NP), NP)
        high = div(p, 4)
        z = (1 - high) * (2 * p) + high * (15 - 2 * p)
        return z * NY + rem(self.y + (dy + NY), NY)

    def row_device(self, dp, dy):
        return (self.row_of(dp, dy), self.col)

    def h_of(self, dh):
        return rem(self.h + (dh + NH), NH)

    def x_of(self, dx):
        return rem(self.x + (dx + NX), NX)

    def col_device(self, dh, dx, dcore):
        core = self.core if dcore == 0 else 1 - self.core
        return (self.row, (self.h_of(dh) * NX + self.x_of(dx)) * 2 + core)

    def slot(self, dh, dx, dcore=0):
        core = self.core if dcore == 0 else 1 - self.core
        return core * (NH * NX) + self.h_of(dh) * NX + self.x_of(dx)

    def row_neighbours(self):
        return [self.row_device(*d) for d in ((1, 0), (-1, 0), (0, 1), (0, -1), (0, 2))]

    def col_neighbours(self):
        steps = ((1, 0, 0), (-1, 0, 0), (0, 1, 0), (0, -1, 0), (0, 2, 0), (0, 0, 1))
        return [self.col_device(*d) for d in steps]


def greet(neighbours):
    barrier = pltpu.get_barrier_semaphore()
    for device in neighbours:
        pl.semaphore_signal(barrier, inc=1, device_id=device, device_id_type=MESH)
    pl.semaphore_wait(barrier, len(neighbours))


class Copy:
    def __init__(self, copy):
        self.copy, self.gone = copy, False
        self.wait_recv = copy.wait_recv

    def left(self):
        if not self.gone:
            self.copy.wait_send()
            self.gone = True


class Wire:
    def __init__(self, send, recv):
        self.send, self.recv, self.started = send, recv, []

    def go(self, src, dst, device):
        n = len(self.started)
        copy = pltpu.make_async_remote_copy(
            src_ref=src,
            dst_ref=dst,
            send_sem=self.send.at[n],
            recv_sem=self.recv.at[n],
            device_id=device,
            device_id_type=MESH,
        )
        copy.start()
        self.started.append(Copy(copy))
        return self.started[-1]

    def drain(self):
        for copy in self.started:
            copy.left()


def halves(rows):
    return pl.ds(0, rows // 2), pl.ds(rows // 2, rows // 2)


GATHER_ROW_COPIES = 14 + 5 * 6 + 3 * 6


def gather_row(wire, at, own, block):
    part = halves(own.shape[0])
    along = (at.row_device(1, 0), at.row_device(-1, 0))
    up, down, far = at.row_device(0, 1), at.row_device(0, -1), at.row_device(0, 2)

    def place(dp, dy, half):
        return block.at[at.row_of(dp, dy), part[half]]

    ends = []

    def spread(dp, half, src, direct):
        dst = place(dp, 0, half)
        a, b = wire.go(src, dst, up), wire.go(src, dst, down)
        if direct:
            ends.extend((a, b, wire.go(src, dst, far)))
            return None
        return dp, half, a, b

    def pass_on(item):
        dp, half, a, b = item
        if half == 0:
            a.wait_recv()
            ref = place(dp, -1, 0)
            ends.extend((b, wire.go(ref, ref, up)))
        else:
            b.wait_recv()
            ref = place(dp, 1, 1)
            ends.extend((a, wire.go(ref, ref, down)))

    moving = {}
    for half in (0, 1):
        for way in (0, 1):
            now = half if way == 0 else 1 - half
            moving[way, now] = wire.go(own.at[part[now]], place(0, 0, now), along[way])
    spreading = [spread(0, half, own.at[part[half]], False) for half in (0, 1)]
    block[at.row_of(0, 0)] = own[...]
    for s in (1, 2, 3, 4):
        now = []
        for half in (0, 1):
            for way in (0, 1):
                part_now = half if way == 0 else 1 - half
                copy = moving.pop((way, part_now), None)
                if copy is None:
                    continue
                copy.wait_recv()
                dp = -s if way == 0 else s
                ref = place(dp, 0, part_now)
                if s < 3 or (s == 3 and part_now == way):
                    moving[way, part_now] = wire.go(ref, ref, along[way])
                now.append(spread(dp, part_now, ref, s >= 3))
        for item in spreading:
            if item is not None:
                pass_on(item)
        spreading = now
    for copy in ends:
        copy.wait_recv()


def add(a, b):
    return (a.astype(F32) + b.astype(F32)).astype(BF16)


SUM_ROW_COPIES = 3 * 3 + 5 * 6 + 14
DIRECT = 3


def sum_row(wire, at, block_of, out, mine, direct_in, first_in, held, second_in, total, z_in, z_out):
    order = (4, 3, -3, 2, -2, 1, -1, 0)
    rows = out.shape[0]
    cut = (slice(0, rows // 2), slice(rows // 2, rows))
    part = halves(rows)
    along = (at.row_device(1, 0), at.row_device(-1, 0))
    up, down, far = at.row_device(0, 1), at.row_device(0, -1), at.row_device(0, 2)
    flight = {}

    def first(i):
        for dy in (2, 1, -1):
            mine[i, dy % NY] = block_of(at.row_of(order[i], dy)).astype(BF16)
        if i > 0:
            for copy in flight[max(0, i - 2)]:
                copy.left()
        if i < DIRECT:
            flight[i] = (
                wire.go(mine.at[i, 2], direct_in.at[i, 2], far),
                wire.go(mine.at[i, 1], direct_in.at[i, 0], up),
                wire.go(mine.at[i, 3], direct_in.at[i, 1], down),
            )
            return
        k = i - DIRECT
        flight[i] = [
            wire.go(mine.at[i, 2, part[0]], first_in.at[k, 0], up),
            wire.go(mine.at[i, 2, part[1]], first_in.at[k, 1], down),
            wire.go(mine.at[i, 1, part[1]], second_in.at[k, 0, part[1]], up),
            wire.go(mine.at[i, 3, part[0]], second_in.at[k, 1, part[0]], down),
        ]

    def second(i):
        k = i - DIRECT
        flight[i][0].wait_recv()
        held[k, 0] = add(mine[i, 1, cut[0]], first_in[k, 0])
        flight[i].append(wire.go(held.at[k, 0], second_in.at[k, 0, part[0]], up))
        flight[i][1].wait_recv()
        held[k, 1] = add(mine[i, 3, cut[1]], first_in[k, 1])
        flight[i].append(wire.go(held.at[k, 1], second_in.at[k, 1, part[1]], down))

    def third(i):
        value = block_of(at.row_of(order[i], 0))
        if i < DIRECT:
            for copy in flight[i]:
                copy.wait_recv()
            for n in range(3):
                value += direct_in[i, n].astype(F32)
        else:
            for copy in flight[i][2:]:
                copy.wait_recv()
            for n in range(2):
                value += second_in[i - DIRECT, n].astype(F32)
        total[i] = value

    moving = {}

    def send(way, half, step):
        moving[way, half] = wire.go(z_out.at[way, half, step], z_in.at[way, half, step], along[way])

    def start(i, way, half, step):
        z_out[way, half, step] = total[i, cut[half]].astype(BF16)
        send(way, half, step)

    def carry(i, way, half, step):
        moving[way, half].wait_recv()
        z_out[way, half, step] = (total[i, cut[half]] + z_in[way, half, step - 1].astype(F32)).astype(BF16)
        send(way, half, step)

    for i in range(3):
        first(i)
    third(0)
    start(0, 0, 0, 0)
    start(0, 1, 1, 0)
    first(3)
    third(1)
    moving[0, 0].left()
    start(1, 0, 1, 1)
    first(4)
    third(2)
    moving[1, 1].left()
    start(2, 1, 0, 1)
    second(3)
    carry(1, 0, 0, 1)
    carry(2, 1, 1, 1)
    first(5)
    second(4)
    first(6)
    third(3)
    third(4)
    first(7)
    for step, i in ((2, 3), (3, 5)):
        for half in (0, 1):
            carry(i, 0, 1 - half, step)
            carry(i + 1, 1, half, step)
        if step == 2:
            for n in (5, 6, 7):
                second(n)
            third(5)
            third(6)
    third(7)
    for half in (0, 1):
        value = total[7, cut[half]]
        for way in (0, 1):
            moving[way, half].wait_recv()
            value += z_in[way, half, 3].astype(F32)
        out[cut[half]] = value.astype(BF16)


def sum_row_scratch(rows, width):
    mid = rows // 2
    return [
        pltpu.VMEM((8, 4, rows, width), BF16),
        pltpu.VMEM((DIRECT, 3, rows, width), BF16),
        pltpu.VMEM((8 - DIRECT, 2, mid, width), BF16),
        pltpu.VMEM((8 - DIRECT, 2, mid, width), BF16),
        pltpu.VMEM((8 - DIRECT, 2, rows, width), BF16),
        pltpu.VMEM((8, rows, width), F32),
        pltpu.VMEM((2, 2, 4, mid, width), BF16),
        pltpu.VMEM((2, 2, 4, mid, width), BF16),
    ]


SUM_COL_COPIES = 4 + 4 * 3 + 6


def sum_col(wire, at, block_of, pair_out, pair_in, paired, x_in, total, z_in, z_out):
    order = (2, 1, -1, 0)
    rows = total.shape[1]
    mid = rows // 2
    cut = (slice(0, mid), slice(mid, rows))
    part = halves(rows)
    along = (at.col_device(1, 0, 0), at.col_device(-1, 0, 0))
    up, down, far = at.col_device(0, 1, 0), at.col_device(0, -1, 0), at.col_device(0, 2, 0)
    other = at.col_device(0, 0, 1)
    crossing, flight = [], []

    def cross(i):
        for dx in range(NX):
            pair_out[i, dx] = block_of(at.slot(order[i], dx, 1)).astype(BF16)
        crossing.append(wire.go(pair_out.at[i], pair_in.at[i], other))

    def first(i):
        crossing[i].wait_recv()
        for dx in (2, 1, 3):
            paired[i, dx] = add(block_of(at.slot(order[i], dx)), pair_in[i, dx])
        if i > 0:
            for copy in flight[max(0, i - 2)]:
                copy.left()
        flight.append(
            [
                wire.go(paired.at[i, dx], x_in.at[i, n], device)
                for dx, n, device in ((2, 2, far), (1, 0, up), (3, 1, down))
            ]
        )

    def third(i):
        value = block_of(at.slot(order[i], 0)) + pair_in[i, 0].astype(F32)
        for copy in flight[i]:
            copy.wait_recv()
        for n in range(3):
            value += x_in[i, n].astype(F32)
        total[i] = value

    moving = {}

    def send(way, half, step):
        moving[way, half] = wire.go(z_out.at[way, half, step], z_in.at[way, half, step], along[way])

    def start(i, way, half, step):
        z_out[way, half, step] = total[i, cut[half]].astype(BF16)
        send(way, half, step)

    def carry(i, way, half, step):
        moving[way, half].wait_recv()
        z_out[way, half, step] = (total[i, cut[half]] + z_in[way, half, step - 1].astype(F32)).astype(BF16)
        send(way, half, step)

    cross(0)
    cross(1)
    first(0)
    cross(2)
    cross(3)
    first(1)
    first(2)
    third(0)
    start(0, 0, 0, 0)
    start(0, 1, 1, 0)
    third(1)
    moving[0, 0].left()
    start(1, 0, 1, 1)
    first(3)
    third(2)
    moving[1, 1].left()
    start(2, 1, 0, 1)
    third(3)
    carry(1, 0, 0, 1)
    carry(2, 1, 1, 1)
    for half in (0, 1):
        value = total[3, cut[half]]
        for way in (0, 1):
            moving[way, half].wait_recv()
            value += z_in[way, half, 1].astype(F32)
        total[3, cut[half]] = value
    return total[3]


def sum_col_scratch(rows, width):
    mid = rows // 2
    return [
        pltpu.VMEM((4, 4, rows, width), BF16),
        pltpu.VMEM((4, 4, rows, width), BF16),
        pltpu.VMEM((4, 4, rows, width), BF16),
        pltpu.VMEM((4, 3, rows, width), BF16),
        pltpu.VMEM((4, rows, width), F32),
        pltpu.VMEM((2, 2, 2, mid, width), BF16),
        pltpu.VMEM((2, 2, 2, mid, width), BF16),
    ]


GATHER_COL_COPIES = 6 + 8 * 3 + 8


def gather_col(wire, at, own, block):
    part = halves(own.shape[0])
    along = (at.col_device(1, 0, 0), at.col_device(-1, 0, 0))
    near = (at.col_device(0, 2, 0), at.col_device(0, 1, 0), at.col_device(0, -1, 0))
    other = at.col_device(0, 0, 1)

    def place(dh, half):
        return block.at[at.slot(dh, 0), part[half]]

    moving = {}
    for way in (0, 1):
        moving[way, way] = wire.go(own.at[part[way]], place(0, way), along[way])
    block[at.slot(0, 0)] = own[...]

    def spread(dh, half):
        ref = place(dh, half)
        return dh, half, [wire.go(ref, ref, device) for device in near]

    crossed = []

    def across(item):
        dh, half, copies = item
        for copy in copies:
            copy.wait_recv()
        first = at.core * (NH * NX) + at.h_of(dh) * NX
        ref = block.at[pl.ds(first, NX), part[half]]
        crossed.append(wire.go(ref, ref, other))

    def arrive(way, half, dh):
        moving[way, half].wait_recv()
        if abs(dh) == 1 and half == way:
            ref = place(dh, half)
            moving[way, half] = wire.go(ref, ref, along[way])
        return spread(dh, half)

    here = [spread(0, half) for half in (0, 1)]
    for item in here:
        across(item)
    for way in (0, 1):
        moving[way, way].left()
        moving[way, 1 - way] = wire.go(own.at[part[1 - way]], place(0, 1 - way), along[way])
    early = [arrive(0, 0, -1), arrive(1, 1, 1)]
    late = [arrive(0, 1, -1), arrive(1, 0, 1)]
    for item in early:
        across(item)
    last = [arrive(0, 0, 2)]
    for item in late:
        across(item)
    last.append(arrive(1, 1, 2))
    for item in last:
        across(item)
    for copy in crossed:
        copy.wait_recv()


def dense(aggregated, weight, out_grad, layer_out):
    v = jnp.dot(aggregated, weight[...], preferred_element_type=F32)
    c, d = 0.7978845608, 0.044715
    th = jnp.tanh(c * (v + d * v * v * v))
    layer_out[...] = (0.5 * v * (1.0 + th)).astype(BF16)
    slope = 0.5 * (1.0 + th) + 0.5 * v * (1.0 - th * th) * (c * (1.0 + (3.0 * d) * v * v))
    pre_grad = (out_grad[...].astype(F32) * slope).astype(BF16)
    return lax.dot_general(
        pre_grad, weight[...], (((1,), (1,)), ((), ())), preferred_element_type=F32
    ).astype(BF16)


def tile_sums(contract, tiles, source, source_at, before, sums):
    slots = tiles.shape[0]
    group = 4

    def some(g, carry):
        for n in range(group):
            k = g * group + n
            product = lax.dot_general(
                tiles[k],
                source[source_at[k]],
                (((contract,), (0,)), ((), ())),
                preferred_element_type=F32,
            )
            sums[k] = product + sums[before[k]]
        return carry

    lax.fori_loop(0, slots // group, some, 0)


def k_plan(rows, cols, count, row_slot, row_before, row_last, col_before, col_last):
    slots = rows.shape[0]

    def clear(t, carry):
        row_last[t] = jnp.int32(slots)
        col_last[t] = jnp.int32(slots)
        return carry

    lax.fori_loop(0, ROWS, clear, 0)

    def slot(k, carry):
        r, c = rows[k], cols[k]
        s = rem(r, 2) * (NH * NX) + div(r, 2)
        row_slot[k] = s
        live = k < count[0]
        old_row, old_col = row_last[s], col_last[c]
        row_before[k], col_before[k] = old_row, old_col
        row_last[s] = jnp.where(live, k, old_row)
        col_last[c] = jnp.where(live, k, old_col)
        return carry

    lax.fori_loop(0, slots, slot, 0)


SMEM_SPEC = pl.BlockSpec(memory_space=pltpu.SMEM)
VMEM_SPEC = pl.BlockSpec(memory_space=pltpu.VMEM)
ANY_SPEC = pl.BlockSpec(memory_space=pl.ANY)
LIMIT = 56 * 1024 * 1024


def plan(rows, cols, count):
    slots = rows.shape[0]
    one = jax.ShapeDtypeStruct((slots,), jnp.int32)
    table = jax.ShapeDtypeStruct((ROWS,), jnp.int32)
    return pl.pallas_call(
        k_plan,
        out_shape=(one, one, table, one, table),
        in_specs=[SMEM_SPEC] * 3,
        out_specs=(SMEM_SPEC,) * 5,
        name="plan",
    )(rows, cols, count)


def k_layer(
    col_at, row_slot, row_before, row_last, col_before, col_last,
    own, tiles_hbm, weight, out_grad, layer_out, grad_x, *scratch
):
    tiles, tile_sem, source, grads, projected, sums, *scratch = scratch
    n_row, n_col = len(sum_row_scratch(32, 128)), len(sum_col_scratch(32, 128))
    row_buffers, col_buffers = scratch[:n_row], scratch[n_row : n_row + n_col]
    send, recv = scratch[n_row + n_col :]
    at = Spot()
    load = pltpu.make_async_copy(tiles_hbm, tiles, tile_sem)
    load.start()
    sums[tiles.shape[0]] = jnp.zeros(sums.shape[1:], F32)
    greet(at.row_neighbours() + at.col_neighbours())
    wire = Wire(send, recv)
    gather_row(wire, at, own, source)
    load.wait()
    tile_sums(1, tiles, source, col_at, row_before, sums)
    aggregated = sum_col(wire, at, lambda slot: sums[row_last[slot]], *col_buffers)
    projected[...] = dense(aggregated.astype(BF16), weight, out_grad, layer_out)
    gather_col(wire, at, projected, grads)
    tile_sums(0, tiles, grads, row_slot, col_before, sums)
    sum_row(wire, at, lambda row: sums[col_last[row]], grad_x, *row_buffers)
    wire.drain()


def layer(tables, own, tiles, weight, out_grad):
    rows, width = own.shape
    slots = tiles.shape[0]
    block = jax.ShapeDtypeStruct((rows, width), BF16)
    copies = GATHER_ROW_COPIES + SUM_COL_COPIES + GATHER_COL_COPIES + SUM_ROW_COPIES
    return pl.pallas_call(
        k_layer,
        out_shape=(block, block),
        in_specs=[SMEM_SPEC] * 6 + [VMEM_SPEC, ANY_SPEC, VMEM_SPEC, VMEM_SPEC],
        out_specs=(VMEM_SPEC, VMEM_SPEC),
        scratch_shapes=[
            pltpu.VMEM(tiles.shape, BF16),
            pltpu.SemaphoreType.DMA,
            pltpu.VMEM((ROWS, rows, width), BF16),
            pltpu.VMEM((COLS, rows, width), BF16),
            pltpu.VMEM((rows, width), BF16),
            pltpu.VMEM((slots + 1, rows, width), F32),
        ]
        + sum_row_scratch(rows, width)
        + sum_col_scratch(rows, width)
        + [pltpu.SemaphoreType.DMA((copies,)), pltpu.SemaphoreType.DMA((copies,))],
        compiler_params=pltpu.CompilerParams(
            collective_id=0, has_side_effects=True, vmem_limit_bytes=LIMIT
        ),
        name="layer",
    )(*tables, own, tiles, weight, out_grad)


def per_device(features, tile_values, tile_rows, tile_cols, tile_count, weight, out_grad):
    rows, cols = tile_rows[0, 0], tile_cols[0, 0]
    tables = plan(rows, cols, tile_count[0])
    return layer((cols,) + tuple(tables), features, tile_values[0, 0], weight, out_grad)


def solution(mesh):
    in_specs = (
        P(("col", "row"), None),
        P("row", "col", None, None, None),
        P("row", "col", None),
        P("row", "col", None),
        P("row", "col"),
        P(),
        P(("row", "col"), None),
    )
    out_specs = (P(("row", "col"), None), P(("col", "row"), None))
    return jax.shard_map(
        per_device, mesh=mesh, in_specs=in_specs, out_specs=out_specs, check_vma=False
    )
```

```python
import jax
import jax.numpy as jnp
from jax import lax
from jax.experimental import pallas as pl
from jax.experimental.pallas import tpu as pltpu
from jax.sharding import PartitionSpec as P

MESH = pl.DeviceIdType.MESH
F32 = jnp.float32
BF16 = jnp.bfloat16
NY, NX, NH, NP = 4, 4, 4, 8
ROWS = NP * NY
COLS = NH * NX * 2


def div(a, b):
    return lax.div(a, jnp.int32(b))


def rem(a, b):
    return lax.rem(a, jnp.int32(b))


class Spot:
    def __init__(self):
        self.row, self.col = lax.axis_index("row"), lax.axis_index("col")
        z = div(self.row, NY)
        odd = rem(z, 2)
        self.p = (1 - odd) * div(z, 2) + odd * div(15 - z, 2)
        self.y = rem(self.row, NY)
        self.h = div(self.col, NX * 2)
        self.x = rem(div(self.col, 2), NX)
        self.core = rem(self.col, 2)

    def row_of(self, dp, dy):
        p = rem(self.p + (dp + NP), NP)
        high = div(p, 4)
        z = (1 - high) * (2 * p) + high * (15 - 2 * p)
        return z * NY + rem(self.y + (dy + NY), NY)

    def row_device(self, dp, dy):
        return (self.row_of(dp, dy), self.col)

    def h_of(self, dh):
        return rem(self.h + (dh + NH), NH)

    def x_of(self, dx):
        return rem(self.x + (dx + NX), NX)

    def col_device(self, dh, dx, dcore):
        core = self.core if dcore == 0 else 1 - self.core
        return (self.row, (self.h_of(dh) * NX + self.x_of(dx)) * 2 + core)

    def slot(self, dh, dx, dcore=0):
        core = self.core if dcore == 0 else 1 - self.core
        return core * (NH * NX) + self.h_of(dh) * NX + self.x_of(dx)

    def row_neighbours(self):
        return [self.row_device(*d) for d in ((1, 0), (-1, 0), (0, 1), (0, -1), (0, 2))]

    def col_neighbours(self):
        steps = ((1, 0, 0), (-1, 0, 0), (0, 1, 0), (0, -1, 0), (0, 2, 0), (0, 0, 1))
        return [self.col_device(*d) for d in steps]


def greet(neighbours):
    barrier = pltpu.get_barrier_semaphore()
    for device in neighbours:
        pl.semaphore_signal(barrier, inc=1, device_id=device, device_id_type=MESH)
    pl.semaphore_wait(barrier, len(neighbours))


class Copy:
    def __init__(self, copy):
        self.copy, self.gone = copy, False
        self.wait_recv = copy.wait_recv

    def left(self):
        if not self.gone:
            self.copy.wait_send()
            self.gone = True


class Wire:
    def __init__(self, send, recv):
        self.send, self.recv, self.started = send, recv, []

    def go(self, src, dst, device):
        n = len(self.started)
        copy = pltpu.make_async_remote_copy(
            src_ref=src,
            dst_ref=dst,
            send_sem=self.send.at[n],
            recv_sem=self.recv.at[n],
            device_id=device,
            device_id_type=MESH,
        )
        copy.start()
        self.started.append(Copy(copy))
        return self.started[-1]

    def drain(self):
        for copy in self.started:
            copy.left()


def halves(rows):
    return pl.ds(0, rows // 2), pl.ds(rows // 2, rows // 2)


GATHER_ROW_COPIES = 14 + 5 * 6 + 3 * 6


def gather_row(wire, at, own, block, meanwhile):
    part = halves(own.shape[0])
    along = (at.row_device(1, 0), at.row_device(-1, 0))
    up, down, far = at.row_device(0, 1), at.row_device(0, -1), at.row_device(0, 2)

    def place(dp, dy, half):
        return block.at[at.row_of(dp, dy), part[half]]

    ends = []

    def spread(dp, half, src, direct):
        dst = place(dp, 0, half)
        a, b = wire.go(src, dst, up), wire.go(src, dst, down)
        if direct:
            ends.extend((a, b, wire.go(src, dst, far)))
            return None
        return dp, half, a, b

    def pass_on(item):
        dp, half, a, b = item
        if half == 0:
            a.wait_recv()
            ref = place(dp, -1, 0)
            ends.extend((b, wire.go(ref, ref, up)))
        else:
            b.wait_recv()
            ref = place(dp, 1, 1)
            ends.extend((a, wire.go(ref, ref, down)))

    moving = {}
    for half in (0, 1):
        for way in (0, 1):
            now = half if way == 0 else 1 - half
            moving[way, now] = wire.go(own.at[part[now]], place(0, 0, now), along[way])
    spreading = [spread(0, half, own.at[part[half]], False) for half in (0, 1)]
    block[at.row_of(0, 0)] = own[...]
    meanwhile()
    for s in (1, 2, 3, 4):
        now = []
        for half in (0, 1):
            for way in (0, 1):
                part_now = half if way == 0 else 1 - half
                copy = moving.pop((way, part_now), None)
                if copy is None:
                    continue
                copy.wait_recv()
                dp = -s if way == 0 else s
                ref = place(dp, 0, part_now)
                if s < 3 or (s == 3 and part_now == way):
                    moving[way, part_now] = wire.go(ref, ref, along[way])
                now.append(spread(dp, part_now, ref, s >= 3))
        for item in spreading:
            if item is not None:
                pass_on(item)
        spreading = now
    for copy in ends:
        copy.wait_recv()


def add(a, b):
    return (a.astype(F32) + b.astype(F32)).astype(BF16)


SUM_ROW_COPIES = 3 * 3 + 5 * 6 + 14
DIRECT = 3


def sum_row(wire, at, block_of, out, mine, direct_in, first_in, held, second_in, total, z_in, z_out):
    order = (4, 3, -3, 2, -2, 1, -1, 0)
    rows = out.shape[0]
    cut = (slice(0, rows // 2), slice(rows // 2, rows))
    part = halves(rows)
    along = (at.row_device(1, 0), at.row_device(-1, 0))
    up, down, far = at.row_device(0, 1), at.row_device(0, -1), at.row_device(0, 2)
    flight = {}

    def first(i):
        for dy in (2, 1, -1):
            mine[i, dy % NY] = block_of(at.row_of(order[i], dy)).astype(BF16)
        if i > 0:
            for copy in flight[max(0, i - 2)]:
                copy.left()
        if i < DIRECT:
            flight[i] = (
                wire.go(mine.at[i, 2], direct_in.at[i, 2], far),
                wire.go(mine.at[i, 1], direct_in.at[i, 0], up),
                wire.go(mine.at[i, 3], direct_in.at[i, 1], down),
            )
            return
        k = i - DIRECT
        flight[i] = [
            wire.go(mine.at[i, 2, part[0]], first_in.at[k, 0], up),
            wire.go(mine.at[i, 2, part[1]], first_in.at[k, 1], down),
            wire.go(mine.at[i, 1, part[1]], second_in.at[k, 0, part[1]], up),
            wire.go(mine.at[i, 3, part[0]], second_in.at[k, 1, part[0]], down),
        ]

    def second(i):
        k = i - DIRECT
        flight[i][0].wait_recv()
        held[k, 0] = add(mine[i, 1, cut[0]], first_in[k, 0])
        flight[i].append(wire.go(held.at[k, 0], second_in.at[k, 0, part[0]], up))
        flight[i][1].wait_recv()
        held[k, 1] = add(mine[i, 3, cut[1]], first_in[k, 1])
        flight[i].append(wire.go(held.at[k, 1], second_in.at[k, 1, part[1]], down))

    def third(i):
        value = block_of(at.row_of(order[i], 0))
        if i < DIRECT:
            for copy in flight[i]:
                copy.wait_recv()
            for n in range(3):
                value += direct_in[i, n].astype(F32)
        else:
            for copy in flight[i][2:]:
                copy.wait_recv()
            for n in range(2):
                value += second_in[i - DIRECT, n].astype(F32)
        total[i] = value

    moving = {}

    def send(way, half, step):
        moving[way, half] = wire.go(z_out.at[way, half, step], z_in.at[way, half, step], along[way])

    def start(i, way, half, step):
        z_out[way, half, step] = total[i, cut[half]].astype(BF16)
        send(way, half, step)

    def carry(i, way, half, step):
        moving[way, half].wait_recv()
        z_out[way, half, step] = (total[i, cut[half]] + z_in[way, half, step - 1].astype(F32)).astype(BF16)
        send(way, half, step)

    for i in range(3):
        first(i)
    third(0)
    start(0, 0, 0, 0)
    start(0, 1, 1, 0)
    first(3)
    third(1)
    moving[0, 0].left()
    start(1, 0, 1, 1)
    first(4)
    third(2)
    moving[1, 1].left()
    start(2, 1, 0, 1)
    second(3)
    carry(1, 0, 0, 1)
    carry(2, 1, 1, 1)
    first(5)
    second(4)
    first(6)
    third(3)
    third(4)
    first(7)
    for step, i in ((2, 3), (3, 5)):
        for half in (0, 1):
            carry(i, 0, 1 - half, step)
            carry(i + 1, 1, half, step)
        if step == 2:
            for n in (5, 6, 7):
                second(n)
            third(5)
            third(6)
    third(7)
    for half in (0, 1):
        value = total[7, cut[half]]
        for way in (0, 1):
            moving[way, half].wait_recv()
            value += z_in[way, half, 3].astype(F32)
        out[cut[half]] = value.astype(BF16)


def sum_row_scratch(rows, width):
    mid = rows // 2
    return [
        pltpu.VMEM((8, 4, rows, width), BF16),
        pltpu.VMEM((DIRECT, 3, rows, width), BF16),
        pltpu.VMEM((8 - DIRECT, 2, mid, width), BF16),
        pltpu.VMEM((8 - DIRECT, 2, mid, width), BF16),
        pltpu.VMEM((8 - DIRECT, 2, rows, width), BF16),
        pltpu.VMEM((8, rows, width), F32),
        pltpu.VMEM((2, 2, 4, mid, width), BF16),
        pltpu.VMEM((2, 2, 4, mid, width), BF16),
    ]


SUM_COL_COPIES = 4 + 4 * 3 + 6


def sum_col(wire, at, block_of, pair_out, pair_in, paired, x_in, total, z_in, z_out):
    order = (2, 1, -1, 0)
    rows = total.shape[1]
    mid = rows // 2
    cut = (slice(0, mid), slice(mid, rows))
    part = halves(rows)
    along = (at.col_device(1, 0, 0), at.col_device(-1, 0, 0))
    up, down, far = at.col_device(0, 1, 0), at.col_device(0, -1, 0), at.col_device(0, 2, 0)
    other = at.col_device(0, 0, 1)
    crossing, flight = [], []

    def cross(i):
        for dx in range(NX):
            pair_out[i, dx] = block_of(at.slot(order[i], dx, 1)).astype(BF16)
        crossing.append(wire.go(pair_out.at[i], pair_in.at[i], other))

    def first(i):
        crossing[i].wait_recv()
        for dx in (2, 1, 3):
            paired[i, dx] = add(block_of(at.slot(order[i], dx)), pair_in[i, dx])
        if i > 0:
            for copy in flight[max(0, i - 2)]:
                copy.left()
        flight.append(
            [
                wire.go(paired.at[i, dx], x_in.at[i, n], device)
                for dx, n, device in ((2, 2, far), (1, 0, up), (3, 1, down))
            ]
        )

    def third(i):
        value = block_of(at.slot(order[i], 0)) + pair_in[i, 0].astype(F32)
        for copy in flight[i]:
            copy.wait_recv()
        for n in range(3):
            value += x_in[i, n].astype(F32)
        total[i] = value

    moving = {}

    def send(way, half, step):
        moving[way, half] = wire.go(z_out.at[way, half, step], z_in.at[way, half, step], along[way])

    def start(i, way, half, step):
        z_out[way, half, step] = total[i, cut[half]].astype(BF16)
        send(way, half, step)

    def carry(i, way, half, step):
        moving[way, half].wait_recv()
        z_out[way, half, step] = (total[i, cut[half]] + z_in[way, half, step - 1].astype(F32)).astype(BF16)
        send(way, half, step)

    cross(0)
    cross(1)
    first(0)
    cross(2)
    cross(3)
    first(1)
    first(2)
    third(0)
    start(0, 0, 0, 0)
    start(0, 1, 1, 0)
    third(1)
    moving[0, 0].left()
    start(1, 0, 1, 1)
    first(3)
    third(2)
    moving[1, 1].left()
    start(2, 1, 0, 1)
    third(3)
    carry(1, 0, 0, 1)
    carry(2, 1, 1, 1)
    for half in (0, 1):
        value = total[3, cut[half]]
        for way in (0, 1):
            moving[way, half].wait_recv()
            value += z_in[way, half, 1].astype(F32)
        total[3, cut[half]] = value
    return total[3]


def sum_col_scratch(rows, width):
    mid = rows // 2
    return [
        pltpu.VMEM((4, 4, rows, width), BF16),
        pltpu.VMEM((4, 4, rows, width), BF16),
        pltpu.VMEM((4, 4, rows, width), BF16),
        pltpu.VMEM((4, 3, rows, width), BF16),
        pltpu.VMEM((4, rows, width), F32),
        pltpu.VMEM((2, 2, 2, mid, width), BF16),
        pltpu.VMEM((2, 2, 2, mid, width), BF16),
    ]


GATHER_COL_COPIES = 6 + 8 * 3 + 8


def gather_col(wire, at, own, block):
    part = halves(own.shape[0])
    along = (at.col_device(1, 0, 0), at.col_device(-1, 0, 0))
    near = (at.col_device(0, 2, 0), at.col_device(0, 1, 0), at.col_device(0, -1, 0))
    other = at.col_device(0, 0, 1)

    def place(dh, half):
        return block.at[at.slot(dh, 0), part[half]]

    moving = {}
    for way in (0, 1):
        moving[way, way] = wire.go(own.at[part[way]], place(0, way), along[way])
    block[at.slot(0, 0)] = own[...]

    def spread(dh, half):
        ref = place(dh, half)
        return dh, half, [wire.go(ref, ref, device) for device in near]

    crossed = []

    def across(item):
        dh, half, copies = item
        for copy in copies:
            copy.wait_recv()
        first = at.core * (NH * NX) + at.h_of(dh) * NX
        ref = block.at[pl.ds(first, NX), part[half]]
        crossed.append(wire.go(ref, ref, other))

    def arrive(way, half, dh):
        moving[way, half].wait_recv()
        if abs(dh) == 1 and half == way:
            ref = place(dh, half)
            moving[way, half] = wire.go(ref, ref, along[way])
        return spread(dh, half)

    here = [spread(0, half) for half in (0, 1)]
    for item in here:
        across(item)
    for way in (0, 1):
        moving[way, way].left()
        moving[way, 1 - way] = wire.go(own.at[part[1 - way]], place(0, 1 - way), along[way])
    early = [arrive(0, 0, -1), arrive(1, 1, 1)]
    late = [arrive(0, 1, -1), arrive(1, 0, 1)]
    for item in early:
        across(item)
    last = [arrive(0, 0, 2)]
    for item in late:
        across(item)
    last.append(arrive(1, 1, 2))
    for item in last:
        across(item)
    for copy in crossed:
        copy.wait_recv()


def dense(aggregated, weight, out_grad, layer_out):
    v = jnp.dot(aggregated, weight[...], preferred_element_type=F32)
    c, d = 0.7978845608, 0.044715
    th = jnp.tanh(c * (v + d * v * v * v))
    layer_out[...] = (0.5 * v * (1.0 + th)).astype(BF16)
    slope = 0.5 * (1.0 + th) + 0.5 * v * (1.0 - th * th) * (c * (1.0 + (3.0 * d) * v * v))
    pre_grad = (out_grad[...].astype(F32) * slope).astype(BF16)
    return lax.dot_general(
        pre_grad, weight[...], (((1,), (1,)), ((), ())), preferred_element_type=F32
    ).astype(BF16)


def tile_sums(contract, tiles, source, source_at, before, sums):
    slots = tiles.shape[0]
    group = 4

    def some(g, carry):
        for n in range(group):
            k = g * group + n
            product = lax.dot_general(
                tiles[k],
                source[source_at(k)],
                (((contract,), (0,)), ((), ())),
                preferred_element_type=F32,
            )
            sums[k] = product + sums[before[k]]
        return carry

    lax.fori_loop(0, slots // group, some, 0)


def slot_tables(targets, count, before, last, target_at):
    slots = targets.shape[0]
    empty = jnp.int32(slots)
    held = [jnp.where(n < count, targets[n], jnp.int32(-1)) for n in range(slots)]

    def one_slot(k, carry):
        own, found = targets[k], empty
        for n in range(slots):
            found = jnp.where((n < k) & (held[n] == own), jnp.int32(n), found)
        before[k] = found
        return carry

    def one_target(t, carry):
        found = empty
        own = target_at(t)
        for n in range(slots):
            found = jnp.where(held[n] == own, jnp.int32(n), found)
        last[t] = found
        return carry

    lax.fori_loop(0, slots, one_slot, 0)
    lax.fori_loop(0, last.shape[0], one_target, 0)


SMEM_SPEC = pl.BlockSpec(memory_space=pltpu.SMEM)
VMEM_SPEC = pl.BlockSpec(memory_space=pltpu.VMEM)
ANY_SPEC = pl.BlockSpec(memory_space=pl.ANY)
LIMIT = 56 * 1024 * 1024


def k_layer(
    row_at, col_at, count, own, tiles_hbm, weight, out_grad, layer_out, grad_x, *scratch
):
    tiles, tile_sem, source, grads, projected, sums, *scratch = scratch
    row_before, row_last, col_before, col_last, *scratch = scratch
    n_row, n_col = len(sum_row_scratch(32, 128)), len(sum_col_scratch(32, 128))
    row_buffers, col_buffers = scratch[:n_row], scratch[n_row : n_row + n_col]
    send, recv = scratch[n_row + n_col :]
    at = Spot()
    load = pltpu.make_async_copy(tiles_hbm, tiles, tile_sem)
    load.start()
    sums[tiles.shape[0]] = jnp.zeros(sums.shape[1:], F32)
    greet(at.row_neighbours() + at.col_neighbours())
    wire = Wire(send, recv)

    def tables():
        slot_tables(row_at, count[0], row_before, row_last, lambda t: rem(t, NH * NX) * 2 + div(t, NH * NX))
        slot_tables(col_at, count[0], col_before, col_last, lambda t: t)

    gather_row(wire, at, own, source, tables)
    load.wait()
    tile_sums(1, tiles, source, lambda k: col_at[k], row_before, sums)
    aggregated = sum_col(wire, at, lambda slot: sums[row_last[slot]], *col_buffers)
    projected[...] = dense(aggregated.astype(BF16), weight, out_grad, layer_out)
    gather_col(wire, at, projected, grads)
    tile_sums(0, tiles, grads, lambda k: rem(row_at[k], 2) * (NH * NX) + div(row_at[k], 2), col_before, sums)
    sum_row(wire, at, lambda row: sums[col_last[row]], grad_x, *row_buffers)
    wire.drain()


def layer(rows_at, cols_at, count, own, tiles, weight, out_grad):
    rows, width = own.shape
    slots = tiles.shape[0]
    block = jax.ShapeDtypeStruct((rows, width), BF16)
    copies = GATHER_ROW_COPIES + SUM_COL_COPIES + GATHER_COL_COPIES + SUM_ROW_COPIES
    return pl.pallas_call(
        k_layer,
        out_shape=(block, block),
        in_specs=[SMEM_SPEC] * 3 + [VMEM_SPEC, ANY_SPEC, VMEM_SPEC, VMEM_SPEC],
        out_specs=(VMEM_SPEC, VMEM_SPEC),
        scratch_shapes=[
            pltpu.VMEM(tiles.shape, BF16),
            pltpu.SemaphoreType.DMA,
            pltpu.VMEM((ROWS, rows, width), BF16),
            pltpu.VMEM((COLS, rows, width), BF16),
            pltpu.VMEM((rows, width), BF16),
            pltpu.VMEM((slots + 1, rows, width), F32),
            pltpu.SMEM((slots,), jnp.int32),
            pltpu.SMEM((COLS,), jnp.int32),
            pltpu.SMEM((slots,), jnp.int32),
            pltpu.SMEM((ROWS,), jnp.int32),
        ]
        + sum_row_scratch(rows, width)
        + sum_col_scratch(rows, width)
        + [pltpu.SemaphoreType.DMA((copies,)), pltpu.SemaphoreType.DMA((copies,))],
        compiler_params=pltpu.CompilerParams(
            collective_id=0, has_side_effects=True, vmem_limit_bytes=LIMIT
        ),
        name="layer",
    )(rows_at, cols_at, count, own, tiles, weight, out_grad)


def per_device(features, tile_values, tile_rows, tile_cols, tile_count, weight, out_grad):
    rows, cols = tile_rows[0, 0], tile_cols[0, 0]
    return layer(rows, cols, tile_count[0], features, tile_values[0, 0], weight, out_grad)


def solution(mesh):
    in_specs = (
        P(("col", "row"), None),
        P("row", "col", None, None, None),
        P("row", "col", None),
        P("row", "col", None),
        P("row", "col"),
        P(),
        P(("row", "col"), None),
    )
    out_specs = (P(("row", "col"), None), P(("col", "row"), None))
    return jax.shard_map(
        per_device, mesh=mesh, in_specs=in_specs, out_specs=out_specs, check_vma=False
    )
```

```python
import jax
import jax.numpy as jnp
from jax import lax
from jax.experimental import pallas as pl
from jax.experimental.pallas import tpu as pltpu
from jax.sharding import PartitionSpec as P

MESH = pl.DeviceIdType.MESH
F32 = jnp.float32
BF16 = jnp.bfloat16
NY, NX, NH, NP = 4, 4, 4, 8
ROWS = NP * NY
COLS = NH * NX * 2


def div(a, b):
    return lax.div(a, jnp.int32(b))


def rem(a, b):
    return lax.rem(a, jnp.int32(b))


class Spot:
    def __init__(self):
        self.row, self.col = lax.axis_index("row"), lax.axis_index("col")
        z = div(self.row, NY)
        odd = rem(z, 2)
        self.p = (1 - odd) * div(z, 2) + odd * div(15 - z, 2)
        self.y = rem(self.row, NY)
        self.h = div(self.col, NX * 2)
        self.x = rem(div(self.col, 2), NX)
        self.core = rem(self.col, 2)

    def row_of(self, dp, dy):
        p = rem(self.p + (dp + NP), NP)
        high = div(p, 4)
        z = (1 - high) * (2 * p) + high * (15 - 2 * p)
        return z * NY + rem(self.y + (dy + NY), NY)

    def row_device(self, dp, dy):
        return (self.row_of(dp, dy), self.col)

    def h_of(self, dh):
        return rem(self.h + (dh + NH), NH)

    def x_of(self, dx):
        return rem(self.x + (dx + NX), NX)

    def col_device(self, dh, dx, dcore):
        core = self.core if dcore == 0 else 1 - self.core
        return (self.row, (self.h_of(dh) * NX + self.x_of(dx)) * 2 + core)

    def slot(self, dh, dx, dcore=0):
        core = self.core if dcore == 0 else 1 - self.core
        return core * (NH * NX) + self.h_of(dh) * NX + self.x_of(dx)

    def row_neighbours(self):
        return [self.row_device(*d) for d in ((1, 0), (-1, 0), (0, 1), (0, -1), (0, 2))]

    def col_neighbours(self):
        steps = ((1, 0, 0), (-1, 0, 0), (0, 1, 0), (0, -1, 0), (0, 2, 0), (0, 0, 1))
        return [self.col_device(*d) for d in steps]


def greet(neighbours):
    barrier = pltpu.get_barrier_semaphore()
    for device in neighbours:
        pl.semaphore_signal(barrier, inc=1, device_id=device, device_id_type=MESH)
    pl.semaphore_wait(barrier, len(neighbours))


class Copy:
    def __init__(self, copy):
        self.copy, self.gone = copy, False
        self.wait_recv = copy.wait_recv

    def left(self):
        if not self.gone:
            self.copy.wait_send()
            self.gone = True


class Wire:
    def __init__(self, send, recv):
        self.send, self.recv, self.started = send, recv, []

    def go(self, src, dst, device):
        n = len(self.started)
        copy = pltpu.make_async_remote_copy(
            src_ref=src,
            dst_ref=dst,
            send_sem=self.send.at[n],
            recv_sem=self.recv.at[n],
            device_id=device,
            device_id_type=MESH,
        )
        copy.start()
        self.started.append(Copy(copy))
        return self.started[-1]

    def drain(self, until=None):
        for copy in self.started[:until]:
            copy.left()


def halves(rows):
    return pl.ds(0, rows // 2), pl.ds(rows // 2, rows // 2)


GATHER_ROW_COPIES = 14 + 5 * 6 + 3 * 6


def gather_row(wire, at, own, block, meanwhile):
    part = halves(own.shape[0])
    along = (at.row_device(1, 0), at.row_device(-1, 0))
    up, down, far = at.row_device(0, 1), at.row_device(0, -1), at.row_device(0, 2)

    def place(dp, dy, half):
        return block.at[at.row_of(dp, dy), part[half]]

    ends = []

    def spread(dp, half, src, direct):
        dst = place(dp, 0, half)
        a, b = wire.go(src, dst, up), wire.go(src, dst, down)
        if direct:
            ends.extend((a, b, wire.go(src, dst, far)))
            return None
        return dp, half, a, b

    def pass_on(item):
        dp, half, a, b = item
        if half == 0:
            a.wait_recv()
            ref = place(dp, -1, 0)
            ends.extend((b, wire.go(ref, ref, up)))
        else:
            b.wait_recv()
            ref = place(dp, 1, 1)
            ends.extend((a, wire.go(ref, ref, down)))

    moving = {}
    for half in (0, 1):
        for way in (0, 1):
            now = half if way == 0 else 1 - half
            moving[way, now] = wire.go(own.at[part[now]], place(0, 0, now), along[way])
    spreading = [spread(0, half, own.at[part[half]], False) for half in (0, 1)]
    block[at.row_of(0, 0)] = own[...]
    meanwhile()
    for s in (1, 2, 3, 4):
        now = []
        for half in (0, 1):
            for way in (0, 1):
                part_now = half if way == 0 else 1 - half
                copy = moving.pop((way, part_now), None)
                if copy is None:
                    continue
                copy.wait_recv()
                dp = -s if way == 0 else s
                ref = place(dp, 0, part_now)
                if s < 3 or (s == 3 and part_now == way):
                    moving[way, part_now] = wire.go(ref, ref, along[way])
                now.append(spread(dp, part_now, ref, s >= 3))
        for item in spreading:
            if item is not None:
                pass_on(item)
        spreading = now
    for copy in ends:
        copy.wait_recv()


def add(a, b):
    return (a.astype(F32) + b.astype(F32)).astype(BF16)


SUM_ROW_COPIES = 3 * 3 + 5 * 6 + 14
DIRECT = 3


def sum_row(wire, at, block_of, out, mine, direct_in, first_in, held, second_in, total, z_in, z_out):
    order = (4, 3, -3, 2, -2, 1, -1, 0)
    rows = out.shape[0]
    cut = (slice(0, rows // 2), slice(rows // 2, rows))
    part = halves(rows)
    along = (at.row_device(1, 0), at.row_device(-1, 0))
    up, down, far = at.row_device(0, 1), at.row_device(0, -1), at.row_device(0, 2)
    flight = {}

    def first(i):
        for dy in (2, 1, -1):
            mine[i, dy % NY] = block_of(at.row_of(order[i], dy)).astype(BF16)
        if i > 0:
            for copy in flight[max(0, i - 2)]:
                copy.left()
        if i < DIRECT:
            flight[i] = (
                wire.go(mine.at[i, 2], direct_in.at[i, 2], far),
                wire.go(mine.at[i, 1], direct_in.at[i, 0], up),
                wire.go(mine.at[i, 3], direct_in.at[i, 1], down),
            )
            return
        k = i - DIRECT
        flight[i] = [
            wire.go(mine.at[i, 2, part[0]], first_in.at[k, 0], up),
            wire.go(mine.at[i, 2, part[1]], first_in.at[k, 1], down),
            wire.go(mine.at[i, 1, part[1]], second_in.at[k, 0, part[1]], up),
            wire.go(mine.at[i, 3, part[0]], second_in.at[k, 1, part[0]], down),
        ]

    def second(i):
        k = i - DIRECT
        flight[i][0].wait_recv()
        held[k, 0] = add(mine[i, 1, cut[0]], first_in[k, 0])
        flight[i].append(wire.go(held.at[k, 0], second_in.at[k, 0, part[0]], up))
        flight[i][1].wait_recv()
        held[k, 1] = add(mine[i, 3, cut[1]], first_in[k, 1])
        flight[i].append(wire.go(held.at[k, 1], second_in.at[k, 1, part[1]], down))

    def third(i):
        value = block_of(at.row_of(order[i], 0))
        if i < DIRECT:
            for copy in flight[i]:
                copy.wait_recv()
            for n in range(3):
                value += direct_in[i, n].astype(F32)
        else:
            for copy in flight[i][2:]:
                copy.wait_recv()
            for n in range(2):
                value += second_in[i - DIRECT, n].astype(F32)
        total[i] = value

    moving = {}

    def send(way, half, step):
        moving[way, half] = wire.go(z_out.at[way, half, step], z_in.at[way, half, step], along[way])

    def start(i, way, half, step):
        z_out[way, half, step] = total[i, cut[half]].astype(BF16)
        send(way, half, step)

    def carry(i, way, half, step):
        moving[way, half].wait_recv()
        z_out[way, half, step] = (total[i, cut[half]] + z_in[way, half, step - 1].astype(F32)).astype(BF16)
        send(way, half, step)

    before = len(wire.started)
    for i in range(3):
        first(i)
    wire.drain(before)
    third(0)
    start(0, 0, 0, 0)
    start(0, 1, 1, 0)
    first(3)
    third(1)
    moving[0, 0].left()
    start(1, 0, 1, 1)
    first(4)
    third(2)
    moving[1, 1].left()
    start(2, 1, 0, 1)
    second(3)
    carry(1, 0, 0, 1)
    carry(2, 1, 1, 1)
    first(5)
    second(4)
    first(6)
    third(3)
    third(4)
    first(7)
    for step, i in ((2, 3), (3, 5)):
        for half in (0, 1):
            carry(i, 0, 1 - half, step)
            carry(i + 1, 1, half, step)
        if step == 2:
            for n in (5, 6, 7):
                second(n)
            third(5)
            third(6)
    third(7)
    for half in (0, 1):
        value = total[7, cut[half]]
        for way in (0, 1):
            moving[way, half].wait_recv()
            value += z_in[way, half, 3].astype(F32)
        out[cut[half]] = value.astype(BF16)


def sum_row_scratch(rows, width):
    mid = rows // 2
    return [
        pltpu.VMEM((8, 4, rows, width), BF16),
        pltpu.VMEM((DIRECT, 3, rows, width), BF16),
        pltpu.VMEM((8 - DIRECT, 2, mid, width), BF16),
        pltpu.VMEM((8 - DIRECT, 2, mid, width), BF16),
        pltpu.VMEM((8 - DIRECT, 2, rows, width), BF16),
        pltpu.VMEM((8, rows, width), F32),
        pltpu.VMEM((2, 2, 4, mid, width), BF16),
        pltpu.VMEM((2, 2, 4, mid, width), BF16),
    ]


SUM_COL_COPIES = 4 + 4 * 3 + 6


def sum_col(wire, at, block_of, pair_out, pair_in, paired, x_in, total, z_in, z_out):
    order = (2, 1, -1, 0)
    rows = total.shape[1]
    mid = rows // 2
    cut = (slice(0, mid), slice(mid, rows))
    part = halves(rows)
    along = (at.col_device(1, 0, 0), at.col_device(-1, 0, 0))
    up, down, far = at.col_device(0, 1, 0), at.col_device(0, -1, 0), at.col_device(0, 2, 0)
    other = at.col_device(0, 0, 1)
    crossing, flight = [], []

    def cross(i):
        for dx in range(NX):
            pair_out[i, dx] = block_of(at.slot(order[i], dx, 1)).astype(BF16)
        crossing.append(wire.go(pair_out.at[i], pair_in.at[i], other))

    def first(i):
        crossing[i].wait_recv()
        for dx in (2, 1, 3):
            paired[i, dx] = add(block_of(at.slot(order[i], dx)), pair_in[i, dx])
        if i > 0:
            for copy in flight[max(0, i - 2)]:
                copy.left()
        flight.append(
            [
                wire.go(paired.at[i, dx], x_in.at[i, n], device)
                for dx, n, device in ((2, 2, far), (1, 0, up), (3, 1, down))
            ]
        )

    def third(i):
        value = block_of(at.slot(order[i], 0)) + pair_in[i, 0].astype(F32)
        for copy in flight[i]:
            copy.wait_recv()
        for n in range(3):
            value += x_in[i, n].astype(F32)
        total[i] = value

    moving = {}

    def send(way, half, step):
        moving[way, half] = wire.go(z_out.at[way, half, step], z_in.at[way, half, step], along[way])

    def start(i, way, half, step):
        z_out[way, half, step] = total[i, cut[half]].astype(BF16)
        send(way, half, step)

    def carry(i, way, half, step):
        moving[way, half].wait_recv()
        z_out[way, half, step] = (total[i, cut[half]] + z_in[way, half, step - 1].astype(F32)).astype(BF16)
        send(way, half, step)

    cross(0)
    cross(1)
    first(0)
    cross(2)
    cross(3)
    first(1)
    first(2)
    third(0)
    start(0, 0, 0, 0)
    start(0, 1, 1, 0)
    third(1)
    moving[0, 0].left()
    start(1, 0, 1, 1)
    first(3)
    third(2)
    moving[1, 1].left()
    start(2, 1, 0, 1)
    third(3)
    carry(1, 0, 0, 1)
    carry(2, 1, 1, 1)
    for half in (0, 1):
        value = total[3, cut[half]]
        for way in (0, 1):
            moving[way, half].wait_recv()
            value += z_in[way, half, 1].astype(F32)
        total[3, cut[half]] = value
    return total[3]


def sum_col_scratch(rows, width):
    mid = rows // 2
    return [
        pltpu.VMEM((4, 4, rows, width), BF16),
        pltpu.VMEM((4, 4, rows, width), BF16),
        pltpu.VMEM((4, 4, rows, width), BF16),
        pltpu.VMEM((4, 3, rows, width), BF16),
        pltpu.VMEM((4, rows, width), F32),
        pltpu.VMEM((2, 2, 2, mid, width), BF16),
        pltpu.VMEM((2, 2, 2, mid, width), BF16),
    ]


GATHER_COL_COPIES = 6 + 8 * 3 + 8


def gather_col(wire, at, own, block):
    part = halves(own.shape[0])
    along = (at.col_device(1, 0, 0), at.col_device(-1, 0, 0))
    near = (at.col_device(0, 2, 0), at.col_device(0, 1, 0), at.col_device(0, -1, 0))
    other = at.col_device(0, 0, 1)

    def place(dh, half):
        return block.at[at.slot(dh, 0), part[half]]

    before = len(wire.started)
    moving = {}
    for way in (0, 1):
        moving[way, way] = wire.go(own.at[part[way]], place(0, way), along[way])
    block[at.slot(0, 0)] = own[...]

    def spread(dh, half):
        ref = place(dh, half)
        return dh, half, [wire.go(ref, ref, device) for device in near]

    crossed = []

    def across(item):
        dh, half, copies = item
        for copy in copies:
            copy.wait_recv()
        first = at.core * (NH * NX) + at.h_of(dh) * NX
        ref = block.at[pl.ds(first, NX), part[half]]
        crossed.append(wire.go(ref, ref, other))

    def arrive(way, half, dh):
        moving[way, half].wait_recv()
        if abs(dh) == 1 and half == way:
            ref = place(dh, half)
            moving[way, half] = wire.go(ref, ref, along[way])
        return spread(dh, half)

    here = [spread(0, half) for half in (0, 1)]
    wire.drain(before)
    for item in here:
        across(item)
    for way in (0, 1):
        moving[way, way].left()
        moving[way, 1 - way] = wire.go(own.at[part[1 - way]], place(0, 1 - way), along[way])
    early = [arrive(0, 0, -1), arrive(1, 1, 1)]
    late = [arrive(0, 1, -1), arrive(1, 0, 1)]
    for item in early:
        across(item)
    last = [arrive(0, 0, 2)]
    for item in late:
        across(item)
    last.append(arrive(1, 1, 2))
    for item in last:
        across(item)
    for copy in crossed:
        copy.wait_recv()


def dense(aggregated, weight, out_grad, layer_out):
    v = jnp.dot(aggregated, weight[...], preferred_element_type=F32)
    c, d = 0.7978845608, 0.044715
    th = jnp.tanh(c * (v + d * v * v * v))
    layer_out[...] = (0.5 * v * (1.0 + th)).astype(BF16)
    slope = 0.5 * (1.0 + th) + 0.5 * v * (1.0 - th * th) * (c * (1.0 + (3.0 * d) * v * v))
    pre_grad = (out_grad[...].astype(F32) * slope).astype(BF16)
    return lax.dot_general(
        pre_grad, weight[...], (((1,), (1,)), ((), ())), preferred_element_type=F32
    ).astype(BF16)


def tile_sums(contract, tiles, source, source_at, before, sums):
    slots = tiles.shape[0]
    group = 4

    def some(g, carry):
        for n in range(group):
            k = g * group + n
            product = lax.dot_general(
                tiles[k],
                source[source_at(k)],
                (((contract,), (0,)), ((), ())),
                preferred_element_type=F32,
            )
            sums[k] = product + sums[before[k]]
        return carry

    lax.fori_loop(0, slots // group, some, 0)


def slot_tables(targets, count, before, last, target_at):
    slots = targets.shape[0]
    empty = jnp.int32(slots)
    held = [jnp.where(n < count, targets[n], jnp.int32(-1)) for n in range(slots)]

    def one_slot(k, carry):
        own, found = targets[k], empty
        for n in range(slots):
            found = jnp.where((n < k) & (held[n] == own), jnp.int32(n), found)
        before[k] = found
        return carry

    def one_target(t, carry):
        found = empty
        own = target_at(t)
        for n in range(slots):
            found = jnp.where(held[n] == own, jnp.int32(n), found)
        last[t] = found
        return carry

    lax.fori_loop(0, slots, one_slot, 0)
    lax.fori_loop(0, last.shape[0], one_target, 0)


SMEM_SPEC = pl.BlockSpec(memory_space=pltpu.SMEM)
VMEM_SPEC = pl.BlockSpec(memory_space=pltpu.VMEM)
ANY_SPEC = pl.BlockSpec(memory_space=pl.ANY)
LIMIT = 56 * 1024 * 1024


def k_layer(
    row_at, col_at, count, own, tiles_hbm, weight, out_grad, layer_out, grad_x, *scratch
):
    tiles, tile_sem, source, grads, projected, sums, *scratch = scratch
    row_before, row_last, col_before, col_last, *scratch = scratch
    n_row, n_col = len(sum_row_scratch(32, 128)), len(sum_col_scratch(32, 128))
    row_buffers, col_buffers = scratch[:n_row], scratch[n_row : n_row + n_col]
    send, recv = scratch[n_row + n_col :]
    at = Spot()
    load = pltpu.make_async_copy(tiles_hbm, tiles, tile_sem)
    load.start()
    sums[tiles.shape[0]] = jnp.zeros(sums.shape[1:], F32)
    greet(at.row_neighbours() + at.col_neighbours())
    wire = Wire(send, recv)

    def tables():
        slot_tables(row_at, count[0], row_before, row_last, lambda t: rem(t, NH * NX) * 2 + div(t, NH * NX))
        slot_tables(col_at, count[0], col_before, col_last, lambda t: t)

    gather_row(wire, at, own, source, tables)
    load.wait()
    tile_sums(1, tiles, source, lambda k: col_at[k], row_before, sums)
    aggregated = sum_col(wire, at, lambda slot: sums[row_last[slot]], *col_buffers)
    projected[...] = dense(aggregated.astype(BF16), weight, out_grad, layer_out)
    gather_col(wire, at, projected, grads)
    tile_sums(0, tiles, grads, lambda k: rem(row_at[k], 2) * (NH * NX) + div(row_at[k], 2), col_before, sums)
    sum_row(wire, at, lambda row: sums[col_last[row]], grad_x, *row_buffers)
    wire.drain()


def layer(rows_at, cols_at, count, own, tiles, weight, out_grad):
    rows, width = own.shape
    slots = tiles.shape[0]
    block = jax.ShapeDtypeStruct((rows, width), BF16)
    copies = GATHER_ROW_COPIES + SUM_COL_COPIES + GATHER_COL_COPIES + SUM_ROW_COPIES
    return pl.pallas_call(
        k_layer,
        out_shape=(block, block),
        in_specs=[SMEM_SPEC] * 3 + [VMEM_SPEC, ANY_SPEC, VMEM_SPEC, VMEM_SPEC],
        out_specs=(VMEM_SPEC, VMEM_SPEC),
        scratch_shapes=[
            pltpu.VMEM(tiles.shape, BF16),
            pltpu.SemaphoreType.DMA,
            pltpu.VMEM((ROWS, rows, width), BF16),
            pltpu.VMEM((COLS, rows, width), BF16),
            pltpu.VMEM((rows, width), BF16),
            pltpu.VMEM((slots + 1, rows, width), F32),
            pltpu.SMEM((slots,), jnp.int32),
            pltpu.SMEM((COLS,), jnp.int32),
            pltpu.SMEM((slots,), jnp.int32),
            pltpu.SMEM((ROWS,), jnp.int32),
        ]
        + sum_row_scratch(rows, width)
        + sum_col_scratch(rows, width)
        + [pltpu.SemaphoreType.DMA((copies,)), pltpu.SemaphoreType.DMA((copies,))],
        compiler_params=pltpu.CompilerParams(
            collective_id=0, has_side_effects=True, vmem_limit_bytes=LIMIT
        ),
        name="layer",
    )(rows_at, cols_at, count, own, tiles, weight, out_grad)


def per_device(features, tile_values, tile_rows, tile_cols, tile_count, weight, out_grad):
    rows, cols = tile_rows[0, 0], tile_cols[0, 0]
    return layer(rows, cols, tile_count[0], features, tile_values[0, 0], weight, out_grad)


def solution(mesh):
    in_specs = (
        P(("col", "row"), None),
        P("row", "col", None, None, None),
        P("row", "col", None),
        P("row", "col", None),
        P("row", "col"),
        P(),
        P(("row", "col"), None),
    )
    out_specs = (P(("row", "col"), None), P(("col", "row"), None))
    return jax.shard_map(
        per_device, mesh=mesh, in_specs=in_specs, out_specs=out_specs, check_vma=False
    )
```
